128 devices in a mesh: frame: 32 (over z, x, core), head: 4 (over y).
Axes of the slice: x: 4, y: 4, z: 4, core: 2. Of those that a mesh axis runs over, the one named last changes fastest.
Arguments:
- queries: bfloat16 [32768, 3072], P(('frame', 'head')), may hold values from -50 to 50
- key_rows: bfloat16 [32768, 3072], P(('frame', 'head')), may hold values from -7 to 7
- value_rows: bfloat16 [32768, 3072], P(('frame', 'head')), may hold values from -12 to 12
- window_mask: int32 [24, 128, 36], P(None, 'frame'), may hold values from 0 to 1, as said below
Outputs:
- attended: bfloat16 [32768, 3072], P(('frame', 'head'))
The draws below stay inside these ranges and needn't reach their ends.
Inputs may be any that keep to these rules, and one draw needn't show every extreme that they name: window_mask[h, i, j] is 1 exactly when key tile j lies inside head h's sliding tile window centred on query tile i: within a head's reach in frame tiles (0 or 1), in tile rows (0 or 1) and in tile columns (0 to 3), cut at the clip's edges; a query tile's own tile is always in, and tiles outside the clip are 0.
All inputs are finite; a program needn't handle non-finite values.
Results may differ from the reference program's by a relative error of at most 0.0032.
Values may be sent and summed in bfloat16 or wider, within the bound.
A program may use at most 256 MiB of HBM per device.

```python
import math
import jax
import jax.numpy as jnp
from jax import lax

H = 24
HEAD_DIM = 128
TILE_TOK = 256
FTILES = 4
COLS_T = 4
ROWS_T = 8
NT = 128
TOKENS = 32768
HD = 3072


def paired_rows(key, spike_rate):
    parts = jax.random.split(key, 7)
    shape = (TOKENS, HD)
    normal_q = jnp.clip(2.5 * jax.random.normal(parts[0], shape, jnp.float32), -12.0, 12.0)
    normal_k = jnp.clip(jax.random.normal(parts[1], shape, jnp.float32), -6.0, 6.0)
    base_q = normal_q
    base_k = normal_k
    order = jnp.arange(TOKENS, dtype=jnp.int32)
    picked = (jax.random.uniform(parts[4], (TOKENS,), jnp.float32) < spike_rate) & (order % 2 == 0)
    strength = jax.random.uniform(parts[5], (TOKENS, 1), jnp.float32, 9.0, 27.0)
    query_out = jnp.where(picked[:, None], strength * base_k, base_q)
    following = jnp.roll(picked, 1)
    jitter = 0.1 * jnp.clip(jax.random.normal(parts[6], shape, jnp.float32), -5.0, 5.0)
    twin_rows = jnp.roll(base_k, 1, axis=0) + jitter
    key_out = jnp.where(following[:, None], twin_rows, base_k)
    return (query_out, key_out)


def draw_queries(key, part):
    query_out, key_out = paired_rows(key, 0.0)
    return query_out.astype(jnp.bfloat16)


def draw_key_rows(key, part):
    query_out, key_out = paired_rows(key, 0.0)
    return key_out.astype(jnp.bfloat16)


def draw_window_mask(key, part):
    key = jax.random.fold_in(key, 11)
    first, second, third = jax.random.split(key, 3)
    ranking = jax.random.permutation(first, H)
    reach_frame = (ranking < 2 * H // 3).astype(jnp.int32)
    row_ranking = jax.random.permutation(second, H)
    reach_row = (row_ranking < H // 2).astype(jnp.int32)
    reach_col = jax.random.randint(third, (H,), 0, 4)
    query_ids = jnp.arange(NT, dtype=jnp.int32)
    query_frame = query_ids // (ROWS_T * COLS_T)
    query_row = query_ids // COLS_T % ROWS_T
    query_col = query_ids % COLS_T
    band_ids = jnp.arange(9 * COLS_T, dtype=jnp.int32)
    frame_step = band_ids // (3 * COLS_T) - 1
    row_step = band_ids // COLS_T % 3 - 1
    key_col = band_ids % COLS_T
    target_frame = query_frame[:, None] + frame_step[None, :]
    target_row = query_row[:, None] + row_step[None, :]
    inside = (target_frame >= 0) & (target_frame < FTILES) & (target_row >= 0) & (target_row < ROWS_T)
    col_gap = jnp.abs(query_col[:, None] - key_col[None, :])
    frame_gap = jnp.abs(frame_step)[None, :]
    row_gap = jnp.abs(row_step)[None, :]
    active = (frame_gap[None] <= reach_frame[:, None, None]) & (row_gap[None] <= reach_row[:, None, None]) & (col_gap[None] <= reach_col[:, None, None]) & inside[None]
    return active.astype(jnp.int32)


def shard_levels(rng, extent, cuts, low, largest):
    def one(dim, shards_of):
        heights = jax.random.uniform(jax.random.fold_in(jax.random.fold_in(rng, 6), dim), (shards_of,), jnp.float32, low / len(cuts), largest / len(cuts))
        return jnp.repeat(jnp.exp(heights), extent[dim] // shards_of).reshape((-1,) + (1,) * (len(extent) - dim - 1))

    loudness = one(*cuts[0])
    for cut in cuts[1:]:
        loudness = loudness * one(*cut)
    return loudness


def centred(key, extent, scale, reach, shards=(), held_as=jnp.bfloat16):
    factor_of = shard_levels(key, extent, shards, -0.22, 0.18) if shards else 1.0
    result = jax.random.normal(key, extent, jnp.float32) * scale * factor_of
    return jnp.minimum(jnp.maximum(result, -reach), reach).astype(held_as)


def setup_inputs(seed: int = 0) -> dict:
    arg_keys = jax.random.split(jax.random.key(seed), 5)
    return {
        "queries": draw_queries(jax.random.fold_in(arg_keys[4], 71), 0),
        "key_rows": draw_key_rows(jax.random.fold_in(arg_keys[4], 71), 0),
        "value_rows": centred(arg_keys[2], (TOKENS, HD), 2.0, 12.0, ((0, 128),)),
        "window_mask": draw_window_mask(jax.random.fold_in(arg_keys[4], 71), 0),
    }


def reference(queries, key_rows, value_rows, window_mask):
    span = COLS_T * TILE_TOK
    rows_all = FTILES * ROWS_T
    scaling = 1.0 / math.sqrt(HEAD_DIM)
    grouped_q = queries.reshape(rows_all, span, H, HEAD_DIM)
    key_value = jnp.stack([key_rows, value_rows], 0).reshape(2, FTILES, ROWS_T, span, H, HEAD_DIM)
    padded = jnp.pad(key_value, ((0, 0), (1, 1), (1, 1), (0, 0), (0, 0), (0, 0)))
    window_band = window_mask.reshape(H, rows_all, COLS_T, 9 * COLS_T)
    zero = jnp.zeros((), jnp.int32)

    def one_row(position):
        frame_pos = (position // ROWS_T).astype(jnp.int32)
        row_pos = (position % ROWS_T).astype(jnp.int32)
        query_row = lax.dynamic_index_in_dim(grouped_q, position, 0, keepdims=False)
        block = lax.dynamic_slice(padded, (zero, frame_pos, row_pos, zero, zero, zero), (2, 3, 3, span, H, HEAD_DIM))
        block = block.reshape(2, 9 * span, H, HEAD_DIM)
        allowed_all = lax.dynamic_index_in_dim(window_band, position, 1, keepdims=False) > 0

        def one_head(head_pos):
            query_head = lax.dynamic_index_in_dim(query_row, head_pos, 1, keepdims=False).astype(jnp.float32)
            key_head = lax.dynamic_index_in_dim(block[0], head_pos, 1, keepdims=False).astype(jnp.float32)
            value_head = lax.dynamic_index_in_dim(block[1], head_pos, 1, keepdims=False).astype(jnp.float32)
            allowed = lax.dynamic_index_in_dim(allowed_all, head_pos, 0, keepdims=False)
            scores = jnp.einsum('qd,kd->qk', query_head, key_head) * scaling
            scores = scores.reshape(COLS_T, TILE_TOK, 9 * COLS_T, TILE_TOK)
            scores = jnp.where(allowed[:, None, :, None], scores, -jnp.inf).reshape(span, 9 * span)
            row_top = lax.optimization_barrier(jnp.max(scores, axis=1, keepdims=True))
            raised = jnp.exp(scores - row_top)
            row_total = lax.optimization_barrier(jnp.sum(raised, axis=1, keepdims=True))
            weights = lax.optimization_barrier(raised.astype(jnp.bfloat16)).astype(jnp.float32)
            return jnp.einsum('qk,kd->qd', weights, value_head) / row_total
        outputs = lax.map(one_head, jnp.arange(H, dtype=jnp.int32))
        return jnp.transpose(outputs, (1, 0, 2)).reshape(span, H * HEAD_DIM).astype(jnp.bfloat16)
    rows_out = lax.map(one_row, jnp.arange(rows_all, dtype=jnp.int32))
    return rows_out.reshape(TOKENS, HD)
```

```python
import functools
import math

import jax
import jax.numpy as jnp
from jax import lax
from jax.experimental import pallas as pl
from jax.experimental.pallas import tpu as pltpu
from jax.sharding import PartitionSpec as P

H = 24
HEAD_DIM = 128
TILE = 256
COLS = 4
ROWS = 8
FTILES = 4
SLOTS = 6
GROUP = 6
SCALE2 = math.log2(math.e) / math.sqrt(HEAD_DIM)
F32 = jnp.float32
BF16 = jnp.bfloat16

LAYOUTS = (
    ((1, 1), (1, 1), (1, 0), (1, 0), (0, 1), (0, 0)),
    ((1, 1), (1, 1), (1, 1), (1, 0), (0, 1), (0, 0)),
    ((1, 1), (1, 1), (1, 1), (1, 1), (1, 1), (1, 1)),
)


def halves(tile):
    turned = jnp.transpose(tile)
    return jnp.concatenate([turned[:, :128], turned[:, 128:]], axis=0)


def pack_kernel(window, q_in, k_in, v_in, pack, order, reach, choice, q_held, k_held, v_held, arrived, count, keys):
    loads = [
        pltpu.make_async_copy(source, held, arrived.at[i])
        for i, (source, held) in enumerate(((q_in, q_held), (k_in, k_held), (v_in, v_held)))
    ]
    for load in loads:
        load.start()

    def clear(i, _):
        count[i] = 0
        return 0

    def measure(h, _):
        sides = [window[h, 0, j] for j in (4, 28, 12, 20)]
        columns = window[h, 0, 16] + window[h, 0, 17] + window[h, 0, 18] + window[h, 0, 19] - 1
        for j, value in enumerate(sides + [columns]):
            reach[h, j] = value
        frame = jnp.maximum(sides[0], sides[1])
        row = jnp.maximum(sides[2], sides[3])
        key = (3 - 2 * frame - row) * COLS + 3 - columns
        keys[h] = key
        count[key + 1] = count[key + 1] + 1
        return 0

    def add_up(i, _):
        count[i + 1] = count[i + 1] + count[i]
        return 0

    def deal(h, fits):
        key = keys[h]
        rank = count[key]
        count[key] = rank + 1
        slot = rank // COLS
        place = lax.rem(rank, COLS)
        lane = jnp.where(lax.rem(slot, 2) == 0, place, COLS - 1 - place)
        order[slot * COLS + lane] = h
        frame = jnp.where(key < 2 * COLS, 1, 0)
        row = jnp.where(lax.rem(key // COLS, 2) == 0, 1, 0)
        held = []
        for number, layout in enumerate(LAYOUTS[:-1]):
            has_frame, has_row = jnp.int32(0), jnp.int32(0)
            for i, (has_f, has_r) in enumerate(layout):
                has_frame = jnp.where(slot == i, has_f, has_frame)
                has_row = jnp.where(slot == i, has_r, has_row)
            short = jnp.maximum(frame - has_frame, row - has_row)
            held.append(jnp.maximum(fits[number], short))
        return tuple(held)

    lax.fori_loop(0, 4 * COLS + 1, clear, 0)
    lax.fori_loop(0, H, measure, 0)
    lax.fori_loop(0, 4 * COLS, add_up, 0)
    short = lax.fori_loop(0, H, deal, (jnp.int32(0),) * (len(LAYOUTS) - 1))
    best = jnp.int32(len(LAYOUTS) - 1)
    for number in reversed(range(len(LAYOUTS) - 1)):
        best = jnp.where(short[number] <= 0, number, best)
    choice[0] = best
    for load in loads:
        load.wait()

    def one(i, _):
        column = pl.ds(pl.multiple_of(order[i] * HEAD_DIM, HEAD_DIM), HEAD_DIM)
        pack[i, 0] = halves(q_held[:, column])
        pack[i, 1] = k_held[:, column]
        pack[i, 2] = halves(v_held[:, column])
        return 0

    lax.fori_loop(0, H, one, 0)


def plan_and_pack(window_mask, queries, key_rows, value_rows):
    smem = pl.BlockSpec(memory_space=pltpu.SMEM)
    any_space = pl.BlockSpec(memory_space=pl.ANY)
    held = pltpu.VMEM((TILE, H * HEAD_DIM), BF16)
    return pl.pallas_call(
        pack_kernel,
        out_shape=(
            jax.ShapeDtypeStruct((H, 3, TILE, HEAD_DIM), BF16),
            jax.ShapeDtypeStruct((H,), jnp.int32),
            jax.ShapeDtypeStruct((H, 5), jnp.int32),
            jax.ShapeDtypeStruct((1,), jnp.int32),
        ),
        in_specs=[smem, any_space, any_space, any_space],
        out_specs=(pl.BlockSpec(memory_space=pltpu.VMEM), smem, smem, smem),
        scratch_shapes=[
            held, held, held,
            pltpu.SemaphoreType.DMA((3,)),
            pltpu.SMEM((4 * COLS + 1,), jnp.int32),
            pltpu.SMEM((H,), jnp.int32),
        ],
        compiler_params=pltpu.CompilerParams(vmem_limit_bytes=60 * 2**20),
        name="pack",
    )(window_mask, queries, key_rows, value_rows)


def exchange_kernel(layout, pack, q_out, kv_out, own_sem, y_send, y_recv, z_send, z_recv, x_send, x_recv):
    frame = lax.axis_index("frame")
    lane = lax.axis_index("head")
    ftile, row = frame // ROWS, lax.rem(frame, ROWS)
    has = {
        ("z", 1): ftile < FTILES - 1,
        ("z", -1): ftile > 0,
        ("x", 1): row < ROWS - 1,
        ("x", -1): row > 0,
    }
    hop = {"z": ROWS, "x": 1}

    def at(axis, way):
        return {"frame": frame + way * hop[axis], "head": lane}

    def across(step):
        return {"frame": frame, "head": lax.rem(lane + step, 4)}

    barrier = pltpu.get_barrier_semaphore()
    for step in (1, 2, 3):
        pl.semaphore_signal(barrier, inc=1, device_id=across(step), device_id_type=pl.DeviceIdType.MESH)
    for (axis, way), there in has.items():
        @pl.when(there)
        def _(axis=axis, way=way):
            pl.semaphore_signal(barrier, inc=1, device_id=at(axis, way), device_id_type=pl.DeviceIdType.MESH)
    peers = jnp.int32(3)
    for there in has.values():
        peers = peers + jnp.where(there, 1, 0)
    pl.semaphore_wait(barrier, peers)

    def own_copies(s):
        return (
            pltpu.make_async_copy(pack.at[s, lane, 0], q_out.at[s, lane], own_sem.at[s, 0]),
            pltpu.make_async_copy(pack.at[s, lane, pl.ds(1, 2)], kv_out.at[s, 1, 1, :, lane], own_sem.at[s, 1]),
        )

    def y_copies(s, step):
        peer = lax.rem(lane + step, 4)
        return (
            pltpu.make_async_remote_copy(
                src_ref=pack.at[s, peer, pl.ds(1, 2)], dst_ref=kv_out.at[s, 1, 1, :, lane],
                send_sem=y_send.at[s, step - 1, 1], recv_sem=y_recv.at[s, step - 1, 1],
                device_id=across(step), device_id_type=pl.DeviceIdType.MESH),
            pltpu.make_async_remote_copy(
                src_ref=pack.at[s, peer, 0], dst_ref=q_out.at[s, lane],
                send_sem=y_send.at[s, step - 1, 0], recv_sem=y_recv.at[s, step - 1, 0],
                device_id=across(step), device_id_type=pl.DeviceIdType.MESH),
        )

    def z_copy(s, way):
        side = 0 if way == 1 else 1
        return pltpu.make_async_remote_copy(
            src_ref=kv_out.at[s, 1, 1], dst_ref=kv_out.at[s, 1 - way, 1],
            send_sem=z_send.at[s, side], recv_sem=z_recv.at[s, side],
            device_id=at("z", way), device_id_type=pl.DeviceIdType.MESH)

    def x_copy(s, f, way):
        side = 0 if way == 1 else 1
        return pltpu.make_async_remote_copy(
            src_ref=kv_out.at[s, f, 1], dst_ref=kv_out.at[s, f, 1 - way],
            send_sem=x_send.at[s, f, side], recv_sem=x_recv.at[s, f, side],
            device_id=at("x", way), device_id_type=pl.DeviceIdType.MESH)

    def present(f):
        return True if f == 1 else has[("z", -1 if f == 0 else 1)]

    def start_y(s):
        for copy in own_copies(s):
            copy.start()
        for step in (1, 3, 2):
            for copy in y_copies(s, step):
                copy.start()

    def wait_y(s):
        for copy in own_copies(s):
            copy.wait()
        for step in (1, 3, 2):
            for copy in y_copies(s, step):
                copy.wait_recv()

    def start_z(s):
        for way in (1, -1):
            @pl.when(has[("z", way)])
            def _(way=way):
                z_copy(s, way).start()

    def wait_z(s):
        for way in (1, -1):
            @pl.when(has[("z", -way)])
            def _(way=way):
                z_copy(s, way).wait_recv()

    def start_x(s, f):
        for way in (1, -1):
            @pl.when(jnp.logical_and(has[("x", way)], present(f)))
            def _(way=way):
                x_copy(s, f, way).start()

    def middle(s):
        if layout[s][0]:
            start_z(s)
        if layout[s][1]:
            start_x(s, 1)

    def corners(s):
        if layout[s][0]:
            wait_z(s)
            if layout[s][1]:
                start_x(s, 0)
                start_x(s, 2)

    for s in range(2):
        start_y(s)
    for s in range(SLOTS):
        wait_y(s)
        if s + 2 < SLOTS:
            start_y(s + 2)
        middle(s)
        if s >= 1:
            corners(s - 1)
    corners(SLOTS - 1)

    for s in range(SLOTS):
        for step in (1, 3, 2):
            for copy in y_copies(s, step):
                copy.wait_send()
        for way in (1, -1):
            if layout[s][0]:
                @pl.when(has[("z", way)])
                def _(s=s, way=way):
                    z_copy(s, way).wait_send()
            if layout[s][1]:
                for f in (0, 1, 2) if layout[s][0] else (1,):
                    @pl.when(jnp.logical_and(has[("x", way)], present(f)))
                    def _(s=s, f=f, way=way):
                        x_copy(s, f, way).wait_send()
                    @pl.when(jnp.logical_and(has[("x", -way)], present(f)))
                    def _(s=s, f=f, way=way):
                        x_copy(s, f, way).wait_recv()


def exchange(number, pack):
    dma = pltpu.SemaphoreType.DMA
    any_space = pl.BlockSpec(memory_space=pl.ANY)
    return pl.pallas_call(
        functools.partial(exchange_kernel, LAYOUTS[number]),
        out_shape=(
            jax.ShapeDtypeStruct((SLOTS, COLS, TILE, HEAD_DIM), BF16),
            jax.ShapeDtypeStruct((SLOTS, 3, 3, 2, COLS, TILE, HEAD_DIM), BF16),
        ),
        in_specs=[any_space],
        out_specs=(any_space, any_space),
        scratch_shapes=[
            dma((SLOTS, 2)),
            dma((SLOTS, 3, 2)),
            dma((SLOTS, 3, 2)),
            dma((SLOTS, 2)),
            dma((SLOTS, 2)),
            dma((SLOTS, 3, 2)),
            dma((SLOTS, 3, 2)),
        ],
        compiler_params=pltpu.CompilerParams(
            collective_id=number, has_side_effects=True
        ),
        name="exchange",
    )(pack.reshape(SLOTS, COLS, 3, TILE, HEAD_DIM))


def attend_kernel(mine, reach, q_ref, kv_ref, o_ref, even, odd, total, top, tiles, live, marks):
    head = mine[pl.program_id(0)]
    f_from, f_to = 1 - reach[head, 0], 2 + reach[head, 1]
    r_from, r_to = 1 - reach[head, 2], 2 + reach[head, 3]
    reach_col = reach[head, 4]
    groups = jnp.int32(0)
    for c in range(COLS):
        c_from, c_to = jnp.maximum(c - reach_col, 0), jnp.minimum(c + reach_col, COLS - 1) + 1

        def over_frames(f, count, c_from=c_from, c_to=c_to):
            def over_rows(r, count):
                def over_columns(column, count):
                    tiles[count] = ((f * 3 + r) * 2 * COLS + column) * TILE
                    live[count] = 1
                    return count + 1
                return lax.fori_loop(c_from, c_to, over_columns, count)
            return lax.fori_loop(r_from, r_to, over_rows, count)

        end = lax.fori_loop(f_from, f_to, over_frames, groups * GROUP)
        after = (end + GROUP - 1) // GROUP
        repeated = tiles[end - 1]

        def fill(i, _, repeated=repeated):
            tiles[i] = repeated
            live[i] = 0
            return 0

        def mark(g, _, c=c, groups=groups, after=after):
            marks[g] = c * 4 + jnp.where(g == groups, 1, 0) + jnp.where(g == after - 1, 2, 0)
            return 0

        lax.fori_loop(end, after * GROUP, fill, 0)
        lax.fori_loop(groups, after, mark, 0)
        groups = after

    def wide(ref, start):
        return jnp.concatenate([ref[0, pl.ds(start, 128), :], ref[0, pl.ds(start + 128, 128), :]], axis=1)

    def scores(g, held):
        q_turned = wide(q_ref, pl.multiple_of((marks[g] // 4) * TILE, TILE))
        largest = None
        for t in range(GROUP):
            start = pl.multiple_of(tiles[g * GROUP + t], TILE)
            part = jnp.dot(kv_ref[0, pl.ds(start, TILE), :], q_turned, preferred_element_type=F32)
            held[t * TILE:(t + 1) * TILE, :] = part
            part = jnp.max(part.reshape(TILE // 8, 8, TILE), axis=0)
            largest = part if largest is None else jnp.maximum(largest, part)
        return jnp.max(largest, axis=0, keepdims=True)

    def phase(g, now, later):
        info = marks[g]
        row_top, fade = top[0:1, :], top[8:9, :]
        following = jnp.minimum(g + 1, groups - 1)
        largest = scores(following, later)
        shift = row_top * SCALE2
        summed = total[...] * fade
        for t in range(GROUP):
            start = pl.multiple_of(tiles[g * GROUP + t] + COLS * TILE, TILE)
            shift_here = jnp.where(live[g * GROUP + t] > 0, shift, jnp.inf)
            weights = jnp.exp2(now[t * TILE:(t + 1) * TILE, :] * SCALE2 - shift_here).astype(BF16)
            values = jnp.concatenate([wide(kv_ref, start), jnp.ones((16, TILE), BF16)], axis=0)
            summed = summed + jnp.dot(values, weights, preferred_element_type=F32)
        total[...] = summed
        starts = lax.rem(marks[following], 2) == 1
        next_top = jnp.where(starts, largest, jnp.maximum(row_top, largest))
        top[0:1, :] = next_top
        top[8:9, :] = jnp.where(starts, 0.0, jnp.exp2((row_top - next_top) * SCALE2))

        @pl.when(lax.rem(info // 2, 2) == 1)
        def _():
            result = summed[:HEAD_DIM] / summed[HEAD_DIM:HEAD_DIM + 1]
            o_ref[0, pl.ds(pl.multiple_of((info // 4) * TILE, TILE), TILE), :] = jnp.transpose(result).astype(BF16)

    top[0:1, :] = scores(0, even)
    top[8:9, :] = jnp.zeros((1, TILE), F32)
    total[...] = jnp.zeros_like(total)

    def pair(i, _):
        phase(2 * i, even, odd)

        @pl.when(2 * i + 1 < groups)
        def _():
            phase(2 * i + 1, odd, even)

        return 0

    lax.fori_loop(0, (groups + 1) // 2, pair, 0)


def attend(mine, reach, moved_q, moved_kv):
    span = COLS * TILE
    return pl.pallas_call(
        attend_kernel,
        grid_spec=pltpu.PrefetchScalarGridSpec(
            num_scalar_prefetch=2,
            grid=(SLOTS,),
            in_specs=[
                pl.BlockSpec((1, span, HEAD_DIM), lambda s, *_: (s, 0, 0)),
                pl.BlockSpec((1, 18 * span, HEAD_DIM), lambda s, *_: (s, 0, 0)),
            ],
            out_specs=pl.BlockSpec((1, span, HEAD_DIM), lambda s, *_: (s, 0, 0)),
            scratch_shapes=[
                pltpu.VMEM((GROUP * TILE, TILE), F32),
                pltpu.VMEM((GROUP * TILE, TILE), F32),
                pltpu.VMEM((HEAD_DIM + 16, TILE), F32),
                pltpu.VMEM((16, TILE), F32),
                pltpu.SMEM((36 * COLS + COLS * GROUP,), jnp.int32),
                pltpu.SMEM((36 * COLS + COLS * GROUP,), jnp.int32),
                pltpu.SMEM((36 * COLS,), jnp.int32),
            ],
        ),
        out_shape=jax.ShapeDtypeStruct((SLOTS, span, HEAD_DIM), BF16),
        compiler_params=pltpu.CompilerParams(vmem_limit_bytes=48 * 2**20),
        name="attend",
    )(mine, reach, moved_q.reshape(SLOTS, span, HEAD_DIM), moved_kv.reshape(SLOTS, 18 * span, HEAD_DIM))


def place_kernel(order, back_ref, o_ref):
    def one(i, _):
        column = pl.ds(pl.multiple_of(order[i] * HEAD_DIM, HEAD_DIM), HEAD_DIM)
        o_ref[:, column] = back_ref[lax.rem(i, 4), i // 4]
        return 0
    lax.fori_loop(0, H, one, 0)


def place(order, back):
    return pl.pallas_call(
        place_kernel,
        out_shape=jax.ShapeDtypeStruct((TILE, H * HEAD_DIM), BF16),
        in_specs=[pl.BlockSpec(memory_space=pltpu.SMEM), pl.BlockSpec(memory_space=pltpu.VMEM)],
        out_specs=pl.BlockSpec(memory_space=pltpu.VMEM),
        name="place",
    )(order, back)


def per_device(queries, key_rows, value_rows, window_mask):
    pack, order, reach, choice = plan_and_pack(window_mask, queries, key_rows, value_rows)
    lane = lax.axis_index("head")
    mine = lax.dynamic_index_in_dim(order.reshape(SLOTS, COLS), lane, 1, keepdims=False)
    moved_q, moved_kv = lax.switch(
        choice[0], [functools.partial(exchange, number) for number in range(len(LAYOUTS))], pack
    )
    attended = attend(mine, reach, moved_q, moved_kv)
    attended = attended.reshape(SLOTS, COLS, TILE, HEAD_DIM).transpose(1, 0, 2, 3)
    back = lax.all_to_all(attended, "head", split_axis=0, concat_axis=0, tiled=True)
    return place(order, back)


def solution(mesh):
    return jax.shard_map(
        per_device,
        mesh=mesh,
        in_specs=(
            P(("frame", "head"), None),
            P(("frame", "head"), None),
            P(("frame", "head"), None),
            P(None, "frame", None),
        ),
        out_specs=P(("frame", "head"), None),
        check_vma=False,
    )
```

```python
import functools
import math

import jax
import jax.numpy as jnp
from jax import lax
from jax.experimental import pallas as pl
from jax.experimental.pallas import tpu as pltpu
from jax.sharding import PartitionSpec as P

H = 24
HEAD_DIM = 128
TILE = 256
COLS = 4
ROWS = 8
FTILES = 4
SLOTS = 6
SCALE2 = math.log2(math.e) / math.sqrt(HEAD_DIM)
F32 = jnp.float32
BF16 = jnp.bfloat16

LAYOUTS = (
    ((1, 1), (1, 1), (1, 0), (1, 0), (0, 1), (0, 0)),
    ((1, 1), (1, 1), (1, 1), (1, 0), (0, 1), (0, 0)),
    ((1, 1), (1, 1), (1, 1), (1, 1), (1, 1), (1, 1)),
)


def halves(tile):
    turned = jnp.transpose(tile)
    return jnp.concatenate([turned[:, :128], turned[:, 128:]], axis=0)


def pack_kernel(window, q_in, k_in, v_in, pack, order, reach, choice, q_held, k_held, v_held, arrived, count, keys, sizes):
    loads = [
        pltpu.make_async_copy(source, held, arrived.at[i])
        for i, (source, held) in enumerate(((q_in, q_held), (k_in, k_held), (v_in, v_held)))
    ]
    for load in loads:
        load.start()

    def clear(i, _):
        count[i] = 0
        return 0

    def measure(h, _):
        sides = [window[h, 0, j] for j in (4, 28, 12, 20)]
        columns = window[h, 0, 16] + window[h, 0, 17] + window[h, 0, 18] + window[h, 0, 19] - 1
        for j, value in enumerate(sides + [columns]):
            sizes[h * 5 + j] = value
        frame = jnp.maximum(sides[0], sides[1])
        row = jnp.maximum(sides[2], sides[3])
        key = (3 - 2 * frame - row) * COLS + 3 - columns
        keys[h] = key
        count[key + 1] = count[key + 1] + 1
        return 0

    def add_up(i, _):
        count[i + 1] = count[i + 1] + count[i]
        return 0

    def deal(h, fits):
        key = keys[h]
        rank = count[key]
        count[key] = rank + 1
        slot = rank // COLS
        place = lax.rem(rank, COLS)
        lane = jnp.where(lax.rem(slot, 2) == 0, place, COLS - 1 - place)
        order[slot * COLS + lane] = h
        frame = jnp.where(key < 2 * COLS, 1, 0)
        row = jnp.where(lax.rem(key // COLS, 2) == 0, 1, 0)
        held = []
        for number, layout in enumerate(LAYOUTS[:-1]):
            has_frame, has_row = jnp.int32(0), jnp.int32(0)
            for i, (has_f, has_r) in enumerate(layout):
                has_frame = jnp.where(slot == i, has_f, has_frame)
                has_row = jnp.where(slot == i, has_r, has_row)
            short = jnp.maximum(frame - has_frame, row - has_row)
            held.append(jnp.maximum(fits[number], short))
        return tuple(held)

    lax.fori_loop(0, 4 * COLS + 1, clear, 0)
    lax.fori_loop(0, H, measure, 0)
    lax.fori_loop(0, 4 * COLS, add_up, 0)
    short = lax.fori_loop(0, H, deal, (jnp.int32(0),) * (len(LAYOUTS) - 1))
    best = jnp.int32(len(LAYOUTS) - 1)
    for number in reversed(range(len(LAYOUTS) - 1)):
        best = jnp.where(short[number] <= 0, number, best)
    choice[0] = best
    lane = lax.axis_index("head")

    def own(s, _):
        for j in range(5):
            reach[s * 5 + j] = sizes[order[s * COLS + lane] * 5 + j]
        return 0

    lax.fori_loop(0, SLOTS, own, 0)
    for load in loads:
        load.wait()

    def one(i, _):
        column = pl.ds(pl.multiple_of(order[i] * HEAD_DIM, HEAD_DIM), HEAD_DIM)
        pack[i, 0] = halves(q_held[:, column])
        pack[i, 1] = k_held[:, column]
        pack[i, 2] = halves(v_held[:, column])
        return 0

    lax.fori_loop(0, H, one, 0)


def plan_and_pack(window_mask, queries, key_rows, value_rows):
    smem = pl.BlockSpec(memory_space=pltpu.SMEM)
    any_space = pl.BlockSpec(memory_space=pl.ANY)
    held = pltpu.VMEM((TILE, H * HEAD_DIM), BF16)
    return pl.pallas_call(
        pack_kernel,
        out_shape=(
            jax.ShapeDtypeStruct((H, 3, TILE, HEAD_DIM), BF16),
            jax.ShapeDtypeStruct((H,), jnp.int32),
            jax.ShapeDtypeStruct((SLOTS * 5,), jnp.int32),
            jax.ShapeDtypeStruct((1,), jnp.int32),
        ),
        in_specs=[smem, any_space, any_space, any_space],
        out_specs=(pl.BlockSpec(memory_space=pltpu.VMEM), smem, smem, smem),
        scratch_shapes=[
            held, held, held,
            pltpu.SemaphoreType.DMA((3,)),
            pltpu.SMEM((4 * COLS + 1,), jnp.int32),
            pltpu.SMEM((H,), jnp.int32),
            pltpu.SMEM((H * 5,), jnp.int32),
        ],
        compiler_params=pltpu.CompilerParams(vmem_limit_bytes=60 * 2**20),
        name="pack",
    )(window_mask, queries, key_rows, value_rows)


def timetable(layout):
    y_time, z_time, x_time, block_time = 8.7, 11.6, 5.8, 1.3
    events, z_free, x_ready = [], 0.0, []
    for s, (has_frame, has_row) in enumerate(layout):
        y_done = y_time * (s + 1) + 1
        events.append((y_done, ("y", s), ((s, 4),)))
        if has_frame:
            z_free = max(z_free, y_done) + z_time
            events.append((z_free, ("z", s), ((s, 1), (s, 7))))
        if has_row:
            x_ready.append((y_done, ("xc", s), ((s, 3), (s, 5)), x_time))
            if has_frame:
                x_ready.append((z_free, ("xk", s), ((s, 0), (s, 2), (s, 6), (s, 8)), 2 * x_time))
    x_free = 0.0
    for ready, name, jobs, length in sorted(x_ready):
        x_free = max(x_free, ready) + length
        events.append((x_free, name, jobs))
    events.sort()
    steps, waits, open_jobs, now = [], [], [], 0.0
    while events or open_jobs:
        while events and (events[0][0] <= now or not open_jobs):
            at, name, jobs = events.pop(0)
            now = max(now, at)
            waits.append(name)
            open_jobs.extend(jobs)
        open_jobs.sort(key=lambda job: (job[0], job[1] != 4))
        steps.append((tuple(waits), open_jobs.pop(0)))
        waits = []
        now += block_time
    return steps


def fused_kernel(
    layout, reach, pack, back, q_held, kv_held, held, total, top, result,
    own_sem, y_send, y_recv, z_send, z_recv, x_send, x_recv, o_own, o_send, o_recv,
):
    frame = lax.axis_index("frame")
    lane = lax.axis_index("head")
    ftile, row = frame // ROWS, lax.rem(frame, ROWS)
    has = {
        ("z", 1): ftile < FTILES - 1,
        ("z", -1): ftile > 0,
        ("x", 1): row < ROWS - 1,
        ("x", -1): row > 0,
    }
    hop = {"z": ROWS, "x": 1}
    mesh_ids = pl.DeviceIdType.MESH
    lanes = (1, 3, 2)

    def at(axis, way):
        return {"frame": frame + way * hop[axis], "head": lane}

    def across(step):
        return {"frame": frame, "head": lax.rem(lane + step, COLS)}

    barrier = pltpu.get_barrier_semaphore()
    for step in lanes:
        pl.semaphore_signal(barrier, inc=1, device_id=across(step), device_id_type=mesh_ids)
    peers = jnp.int32(3)
    for (axis, way), there in has.items():
        peers = peers + jnp.where(there, 1, 0)

        @pl.when(there)
        def _(axis=axis, way=way):
            pl.semaphore_signal(barrier, inc=1, device_id=at(axis, way), device_id_type=mesh_ids)
    pl.semaphore_wait(barrier, peers)

    def own_copies(s):
        return (
            pltpu.make_async_copy(pack.at[s, lane, 0], q_held.at[s * COLS + lane], own_sem.at[s, 0]),
            pltpu.make_async_copy(pack.at[s, lane, pl.ds(1, 2)], kv_held.at[s * 9 + 4, :, lane], own_sem.at[s, 1]),
        )

    def y_copies(s, step):
        peer = lax.rem(lane + step, COLS)
        return (
            pltpu.make_async_remote_copy(
                src_ref=pack.at[s, peer, pl.ds(1, 2)], dst_ref=kv_held.at[s * 9 + 4, :, lane],
                send_sem=y_send.at[s, step - 1, 1], recv_sem=y_recv.at[s, step - 1, 1],
                device_id=across(step), device_id_type=mesh_ids),
            pltpu.make_async_remote_copy(
                src_ref=pack.at[s, peer, 0], dst_ref=q_held.at[s * COLS + lane],
                send_sem=y_send.at[s, step - 1, 0], recv_sem=y_recv.at[s, step - 1, 0],
                device_id=across(step), device_id_type=mesh_ids),
        )

    def z_copy(s, way):
        side = 0 if way == 1 else 1
        return pltpu.make_async_remote_copy(
            src_ref=kv_held.at[s * 9 + 4], dst_ref=kv_held.at[s * 9 + (1 - way) * 3 + 1],
            send_sem=z_send.at[s, side], recv_sem=z_recv.at[s, side],
            device_id=at("z", way), device_id_type=mesh_ids)

    def x_copy(s, f, way):
        side = 0 if way == 1 else 1
        return pltpu.make_async_remote_copy(
            src_ref=kv_held.at[s * 9 + f * 3 + 1], dst_ref=kv_held.at[s * 9 + f * 3 + 1 - way],
            send_sem=x_send.at[s, f, side], recv_sem=x_recv.at[s, f, side],
            device_id=at("x", way), device_id_type=mesh_ids)

    def o_copy(s, step):
        peer = lax.rem(lane + step, COLS)
        return pltpu.make_async_remote_copy(
            src_ref=result.at[s * COLS + peer], dst_ref=back.at[s * COLS + lane],
            send_sem=o_send.at[s, step - 1], recv_sem=o_recv.at[s, step - 1],
            device_id=across(step), device_id_type=mesh_ids)

    def o_keep(s):
        return pltpu.make_async_copy(result.at[s * COLS + lane], back.at[s * COLS + lane], o_own.at[s])

    def present(f):
        return True if f == 1 else has[("z", -1 if f == 0 else 1)]

    def when_row(f, way, act):
        @pl.when(jnp.logical_and(has[("x", way)], present(f)))
        def _():
            act()

    def start_y(s):
        for copy in own_copies(s):
            copy.start()
        for step in lanes:
            for copy in y_copies(s, step):
                copy.start()

    def wait(kind, s):
        has_frame, has_row = layout[s]
        if kind == "y":
            for copy in own_copies(s):
                copy.wait()
            for step in lanes:
                for copy in y_copies(s, step):
                    copy.wait_recv()
            if s + 2 < SLOTS:
                start_y(s + 2)
            for way in (1, -1):
                if has_frame:
                    @pl.when(has[("z", way)])
                    def _(way=way):
                        z_copy(s, way).start()
                if has_row:
                    when_row(1, way, lambda way=way: x_copy(s, 1, way).start())
        elif kind == "z":
            for way in (1, -1):
                @pl.when(has[("z", -way)])
                def _(way=way):
                    z_copy(s, way).wait_recv()
            if has_row:
                for f in (0, 2):
                    for way in (1, -1):
                        when_row(f, way, lambda f=f, way=way: x_copy(s, f, way).start())
        else:
            for f in (1,) if kind == "xc" else (0, 2):
                for way in (1, -1):
                    when_row(f, -way, lambda f=f, way=way: x_copy(s, f, way).wait_recv())

    def wide(tile):
        return jnp.concatenate([tile[:128], tile[128:]], axis=1)

    def first(s, c, block, allowed):
        q_turned = wide(q_held[s * COLS + c])
        largest = None
        for t in range(COLS):
            part = jnp.dot(kv_held[block, 0, t], q_turned, preferred_element_type=F32)
            held[c, t * TILE:(t + 1) * TILE, :] = part
            part = jnp.max(part.reshape(TILE // 8, 8, TILE), axis=0)
            part = jnp.where(allowed[abs(t - c)], part, -jnp.inf)
            largest = part if largest is None else jnp.maximum(largest, part)
        return jnp.max(largest, axis=0, keepdims=True)

    def second(s, c, block, allowed, largest, fresh):
        item = s * COLS + c
        before = jnp.where(fresh, -1e30, top[item, 0:1, :])
        row_top = jnp.maximum(before, largest)
        shift = row_top * SCALE2
        summed = jnp.where(fresh, 0.0, total[item]) * jnp.exp2((before - row_top) * SCALE2)
        for t in range(COLS):
            shift_here = jnp.where(allowed[abs(t - c)], shift, jnp.inf)
            weights = jnp.exp2(held[c, t * TILE:(t + 1) * TILE, :] * SCALE2 - shift_here).astype(BF16)
            values = jnp.concatenate([wide(kv_held[block, 1, t]), jnp.ones((16, TILE), BF16)], axis=0)
            summed = summed + jnp.dot(values, weights, preferred_element_type=F32)
        total[item] = summed
        top[item, 0:1, :] = row_top

    def attend_block(s, b):
        f, r = b // 3, lax.rem(b, 3)
        inside = jnp.logical_and(
            jnp.logical_and(ftile + f >= 1, ftile + f <= FTILES), jnp.logical_and(row + r >= 1, row + r <= ROWS))

        @pl.when(inside)
        def _():
            base = s * 5
            flag = jnp.where(f == 1, 1, jnp.where(f == 0, reach[base], reach[base + 1]))
            flag = flag * jnp.where(r == 1, 1, jnp.where(r == 0, reach[base + 2], reach[base + 3]))
            columns = jnp.where(flag > 0, reach[base + 4], -1)
            allowed = [columns >= gap for gap in range(COLS)]
            block = s * 9 + b
            fresh = b == 4
            largest = first(s, 0, block, allowed)
            for c in range(COLS):
                following = first(s, c + 1, block, allowed) if c + 1 < COLS else None
                second(s, c, block, allowed, largest, fresh)
                largest = following

    steps = timetable(layout)
    last_of = {s: i for i, (_, (s, _)) in enumerate(steps)}

    def pick(i, values):
        chosen = jnp.int32(values[0])
        for number, value in enumerate(values):
            if number and value != values[0]:
                chosen = jnp.where(i == number, value, chosen)
        return chosen

    def run_step(i, _):
        for number, (waits, _) in enumerate(steps):
            if waits:
                @pl.when(i == number)
                def _(waits=waits):
                    for kind, s in waits:
                        wait(kind, s)
        s = pick(i, [job[0] for _, job in steps])
        attend_block(s, pick(i, [job[1] for _, job in steps]))

        @pl.when(pick(i, [int(last_of[job[0]] == number) for number, (_, job) in enumerate(steps)]) == 1)
        def _():
            for c in range(COLS):
                summed = total[s * COLS + c]
                blended = summed[:HEAD_DIM] / summed[HEAD_DIM:HEAD_DIM + 1]
                result[s * COLS + c] = jnp.transpose(blended).astype(BF16)
            o_keep(s).start()
            for step in lanes:
                o_copy(s, step).start()
        return 0

    start_y(0)
    start_y(1)
    lax.fori_loop(0, len(steps), run_step, 0)

    for s, (has_frame, has_row) in enumerate(layout):
        o_keep(s).wait()
        for step in lanes:
            o_copy(s, step).wait()
            for copy in y_copies(s, step):
                copy.wait_send()
        for way in (1, -1):
            if has_frame:
                @pl.when(has[("z", way)])
                def _(s=s, way=way):
                    z_copy(s, way).wait_send()
            if has_row:
                for f in (0, 1, 2) if has_frame else (1,):
                    when_row(f, way, lambda s=s, f=f, way=way: x_copy(s, f, way).wait_send())


def fused(number, reach, pack):
    dma = pltpu.SemaphoreType.DMA
    any_space = pl.BlockSpec(memory_space=pl.ANY)
    items = SLOTS * COLS
    return pl.pallas_call(
        functools.partial(fused_kernel, LAYOUTS[number]),
        out_shape=jax.ShapeDtypeStruct((items, TILE, HEAD_DIM), BF16),
        in_specs=[pl.BlockSpec(memory_space=pltpu.SMEM), any_space],
        out_specs=any_space,
        scratch_shapes=[
            pltpu.VMEM((items, TILE, HEAD_DIM), BF16),
            pltpu.VMEM((SLOTS * 9, 2, COLS, TILE, HEAD_DIM), BF16),
            pltpu.VMEM((COLS, COLS * TILE, TILE), F32),
            pltpu.VMEM((items, HEAD_DIM + 16, TILE), F32),
            pltpu.VMEM((items, 8, TILE), F32),
            pltpu.VMEM((items, TILE, HEAD_DIM), BF16),
            dma((SLOTS, 2)),
            dma((SLOTS, 3, 2)),
            dma((SLOTS, 3, 2)),
            dma((SLOTS, 2)),
            dma((SLOTS, 2)),
            dma((SLOTS, 3, 2)),
            dma((SLOTS, 3, 2)),
            dma((SLOTS,)),
            dma((SLOTS, 3)),
            dma((SLOTS, 3)),
        ],
        compiler_params=pltpu.CompilerParams(
            collective_id=number, has_side_effects=True, vmem_limit_bytes=56 * 2**20
        ),
        name="fused",
    )(reach, pack.reshape(SLOTS, COLS, 3, TILE, HEAD_DIM))


def place_kernel(order, back_ref, o_ref):
    def one(i, _):
        column = pl.ds(pl.multiple_of(order[i] * HEAD_DIM, HEAD_DIM), HEAD_DIM)
        o_ref[:, column] = back_ref[i]
        return 0
    lax.fori_loop(0, H, one, 0)


def place(order, back):
    return pl.pallas_call(
        place_kernel,
        out_shape=jax.ShapeDtypeStruct((TILE, H * HEAD_DIM), BF16),
        in_specs=[pl.BlockSpec(memory_space=pltpu.SMEM), pl.BlockSpec(memory_space=pltpu.VMEM)],
        out_specs=pl.BlockSpec(memory_space=pltpu.VMEM),
        name="place",
    )(order, back)


def per_device(queries, key_rows, value_rows, window_mask):
    pack, order, reach, choice = plan_and_pack(window_mask, queries, key_rows, value_rows)
    back = lax.switch(
        choice[0], [functools.partial(fused, number) for number in range(len(LAYOUTS))], reach, pack
    )
    return place(order, back)


def solution(mesh):
    return jax.shard_map(
        per_device,
        mesh=mesh,
        in_specs=(
            P(("frame", "head"), None),
            P(("frame", "head"), None),
            P(("frame", "head"), None),
            P(None, "frame", None),
        ),
        out_specs=P(("frame", "head"), None),
        check_vma=False,
    )
```

```python
import functools
import math

import jax
import jax.numpy as jnp
from jax import lax
from jax.experimental import pallas as pl
from jax.experimental.pallas import tpu as pltpu
from jax.sharding import PartitionSpec as P

H = 24
HEAD_DIM = 128
TILE = 256
COLS = 4
ROWS = 8
FTILES = 4
SLOTS = 6
SCALE2 = math.log2(math.e) / math.sqrt(HEAD_DIM)
F32 = jnp.float32
BF16 = jnp.bfloat16

LAYOUTS = (
    ((1, 1), (1, 1), (1, 0), (1, 0), (0, 1), (0, 0)),
    ((1, 1), (1, 1), (1, 1), (1, 0), (0, 1), (0, 0)),
    ((1, 1), (1, 1), (1, 1), (1, 1), (1, 1), (1, 1)),
)


def halves(tile):
    turned = jnp.transpose(tile)
    return jnp.concatenate([turned[:, :128], turned[:, 128:]], axis=0)


def plan_kernel(window, order, reach, choice, count, keys, sizes):
    def clear(i, _):
        count[i] = 0
        return 0

    def measure(h, _):
        sides = [window[h, 0, j] for j in (4, 28, 12, 20)]
        columns = window[h, 0, 16] + window[h, 0, 17] + window[h, 0, 18] + window[h, 0, 19] - 1
        for j, value in enumerate(sides + [columns]):
            sizes[h * 5 + j] = value
        frame = jnp.maximum(sides[0], sides[1])
        row = jnp.maximum(sides[2], sides[3])
        key = (3 - 2 * frame - row) * COLS + 3 - columns
        keys[h] = key
        count[key + 1] = count[key + 1] + 1
        return 0

    def add_up(i, _):
        count[i + 1] = count[i + 1] + count[i]
        return 0

    def deal(h, fits):
        key = keys[h]
        rank = count[key]
        count[key] = rank + 1
        slot = rank // COLS
        place = lax.rem(rank, COLS)
        lane = jnp.where(lax.rem(slot, 2) == 0, place, COLS - 1 - place)
        order[slot * COLS + lane] = h
        frame = jnp.where(key < 2 * COLS, 1, 0)
        row = jnp.where(lax.rem(key // COLS, 2) == 0, 1, 0)
        held = []
        for number, layout in enumerate(LAYOUTS[:-1]):
            has_frame, has_row = jnp.int32(0), jnp.int32(0)
            for i, (has_f, has_r) in enumerate(layout):
                has_frame = jnp.where(slot == i, has_f, has_frame)
                has_row = jnp.where(slot == i, has_r, has_row)
            short = jnp.maximum(frame - has_frame, row - has_row)
            held.append(jnp.maximum(fits[number], short))
        return tuple(held)

    lax.fori_loop(0, 4 * COLS + 1, clear, 0)
    lax.fori_loop(0, H, measure, 0)
    lax.fori_loop(0, 4 * COLS, add_up, 0)
    short = lax.fori_loop(0, H, deal, (jnp.int32(0),) * (len(LAYOUTS) - 1))
    best = jnp.int32(len(LAYOUTS) - 1)
    for number in reversed(range(len(LAYOUTS) - 1)):
        best = jnp.where(short[number] <= 0, number, best)
    choice[0] = best
    lane = lax.axis_index("head")

    def own(s, _):
        for j in range(5):
            reach[s * 5 + j] = sizes[order[s * COLS + lane] * 5 + j]
        return 0

    lax.fori_loop(0, SLOTS, own, 0)
    for j in range(5):
        reach[SLOTS * 5 + j] = 0


def make_plan(window_mask):
    smem = pl.BlockSpec(memory_space=pltpu.SMEM)
    return pl.pallas_call(
        plan_kernel,
        out_shape=(
            jax.ShapeDtypeStruct((H,), jnp.int32),
            jax.ShapeDtypeStruct((SLOTS * 5 + 5,), jnp.int32),
            jax.ShapeDtypeStruct((1,), jnp.int32),
        ),
        in_specs=[smem],
        out_specs=(smem, smem, smem),
        scratch_shapes=[
            pltpu.SMEM((4 * COLS + 1,), jnp.int32),
            pltpu.SMEM((H,), jnp.int32),
            pltpu.SMEM((H * 5,), jnp.int32),
        ],
        name="plan",
    )(window_mask)


def timetable(layout):
    y_time, z_time, x_time, block_time = 8.7, 11.6, 5.8, 1.3
    events, z_free, x_ready = [], 0.0, []
    for s, (has_frame, has_row) in enumerate(layout):
        y_done = y_time * (s + 1) + 1
        events.append((y_done, ("y", s), ((s, 4),)))
        if has_frame:
            z_free = max(z_free, y_done) + z_time
            events.append((z_free, ("z", s), ((s, 1), (s, 7))))
        if has_row:
            x_ready.append((y_done, ("xc", s), ((s, 3), (s, 5)), x_time))
            if has_frame:
                x_ready.append((z_free, ("xk", s), ((s, 0), (s, 2), (s, 6), (s, 8)), 2 * x_time))
    x_free = 0.0
    for ready, name, jobs, length in sorted(x_ready):
        x_free = max(x_free, ready) + length
        events.append((x_free, name, jobs))
    events.sort()
    steps, waits, open_jobs, now = [], [], [], 0.0
    while events or open_jobs:
        while events and (events[0][0] <= now or not open_jobs):
            at, name, jobs = events.pop(0)
            now = max(now, at)
            waits.append(name)
            open_jobs.extend(jobs)
        open_jobs.sort(key=lambda job: (job[0], job[1] != 4))
        steps.append((tuple(waits), open_jobs.pop(0)))
        waits = []
        now += block_time
    return steps


def fused_kernel(
    layout, order, reach, q_in, k_in, v_in, back, raw, pack, q_held, kv_held, held, total, top, waiting, result,
    raw_sem, own_sem, y_send, y_recv, z_send, z_recv, x_send, x_recv, o_own, o_send, o_recv,
):
    frame = lax.axis_index("frame")
    lane = lax.axis_index("head")
    ftile, row = frame // ROWS, lax.rem(frame, ROWS)
    has = {
        ("z", 1): ftile < FTILES - 1,
        ("z", -1): ftile > 0,
        ("x", 1): row < ROWS - 1,
        ("x", -1): row > 0,
    }
    hop = {"z": ROWS, "x": 1}
    mesh_ids = pl.DeviceIdType.MESH
    lanes = (1, 3, 2)

    def at(axis, way):
        return {"frame": frame + way * hop[axis], "head": lane}

    def across(step):
        return {"frame": frame, "head": lax.rem(lane + step, COLS)}

    barrier = pltpu.get_barrier_semaphore()
    for step in lanes:
        pl.semaphore_signal(barrier, inc=1, device_id=across(step), device_id_type=mesh_ids)
    peers = jnp.int32(3)
    for (axis, way), there in has.items():
        peers = peers + jnp.where(there, 1, 0)

        @pl.when(there)
        def _(axis=axis, way=way):
            pl.semaphore_signal(barrier, inc=1, device_id=at(axis, way), device_id_type=mesh_ids)

    def raw_copies(h):
        column = pl.ds(pl.multiple_of(h * HEAD_DIM, HEAD_DIM), HEAD_DIM)
        return [
            pltpu.make_async_copy(source.at[:, column], raw.at[i, h], raw_sem.at[i, h])
            for i, source in enumerate((q_in, k_in, v_in))
        ]

    def load_raw(h, _):
        for copy in raw_copies(h):
            copy.start()
        return 0

    def wait_raw(h, _):
        for copy in raw_copies(h):
            copy.wait()
        return 0

    def pack_slot(s):
        def one(y, _):
            head = order[s * COLS + y]
            pack[s, y, 0] = halves(raw[0, head])
            pack[s, y, 1] = raw[1, head]
            pack[s, y, 2] = halves(raw[2, head])
            return 0

        lax.fori_loop(0, COLS, one, 0)

    def own_copies(s):
        return (
            pltpu.make_async_copy(pack.at[s, lane, 0], q_held.at[s * COLS + lane], own_sem.at[s, 0]),
            pltpu.make_async_copy(pack.at[s, lane, pl.ds(1, 2)], kv_held.at[s * 9 + 4, :, lane], own_sem.at[s, 1]),
        )

    def y_copies(s, step):
        peer = lax.rem(lane + step, COLS)
        return (
            pltpu.make_async_remote_copy(
                src_ref=pack.at[s, peer, pl.ds(1, 2)], dst_ref=kv_held.at[s * 9 + 4, :, lane],
                send_sem=y_send.at[s, step - 1, 1], recv_sem=y_recv.at[s, step - 1, 1],
                device_id=across(step), device_id_type=mesh_ids),
            pltpu.make_async_remote_copy(
                src_ref=pack.at[s, peer, 0], dst_ref=q_held.at[s * COLS + lane],
                send_sem=y_send.at[s, step - 1, 0], recv_sem=y_recv.at[s, step - 1, 0],
                device_id=across(step), device_id_type=mesh_ids),
        )

    def z_copy(s, way):
        side = 0 if way == 1 else 1
        return pltpu.make_async_remote_copy(
            src_ref=kv_held.at[s * 9 + 4], dst_ref=kv_held.at[s * 9 + (1 - way) * 3 + 1],
            send_sem=z_send.at[s, side], recv_sem=z_recv.at[s, side],
            device_id=at("z", way), device_id_type=mesh_ids)

    def x_copy(s, f, way):
        side = 0 if way == 1 else 1
        return pltpu.make_async_remote_copy(
            src_ref=kv_held.at[s * 9 + f * 3 + 1], dst_ref=kv_held.at[s * 9 + f * 3 + 1 - way],
            send_sem=x_send.at[s, f, side], recv_sem=x_recv.at[s, f, side],
            device_id=at("x", way), device_id_type=mesh_ids)

    def o_copy(s, step):
        peer = lax.rem(lane + step, COLS)
        return pltpu.make_async_remote_copy(
            src_ref=result.at[s * COLS + peer], dst_ref=back.at[s * COLS + lane],
            send_sem=o_send.at[s, step - 1], recv_sem=o_recv.at[s, step - 1],
            device_id=across(step), device_id_type=mesh_ids)

    def o_keep(s):
        return pltpu.make_async_copy(result.at[s * COLS + lane], back.at[s * COLS + lane], o_own.at[s])

    def present(f):
        return True if f == 1 else has[("z", -1 if f == 0 else 1)]

    def when_row(f, way, act):
        @pl.when(jnp.logical_and(has[("x", way)], present(f)))
        def _():
            act()

    def start_y(s):
        for copy in own_copies(s):
            copy.start()
        for step in lanes:
            for copy in y_copies(s, step):
                copy.start()

    def wait(kind, s):
        has_frame, has_row = layout[s]
        if kind == "y":
            for copy in own_copies(s):
                copy.wait()
            for step in lanes:
                for copy in y_copies(s, step):
                    copy.wait_recv()
            if s + 2 < SLOTS:
                start_y(s + 2)
            for way in (1, -1):
                if has_frame:
                    @pl.when(has[("z", way)])
                    def _(way=way):
                        z_copy(s, way).start()
                if has_row:
                    when_row(1, way, lambda way=way: x_copy(s, 1, way).start())
        elif kind == "z":
            for way in (1, -1):
                @pl.when(has[("z", -way)])
                def _(way=way):
                    z_copy(s, way).wait_recv()
            if has_row:
                for f in (0, 2):
                    for way in (1, -1):
                        when_row(f, way, lambda f=f, way=way: x_copy(s, f, way).start())
        else:
            for f in (1,) if kind == "xc" else (0, 2):
                for way in (1, -1):
                    when_row(f, -way, lambda f=f, way=way: x_copy(s, f, way).wait_recv())

    def wide(tile):
        return jnp.concatenate([tile[:128], tile[128:]], axis=1)

    def first(s, c, block, allowed):
        q_turned = wide(q_held[s * COLS + c])
        largest = None
        for t in range(COLS):
            part = jnp.dot(kv_held[block, 0, t], q_turned, preferred_element_type=F32)
            held[c, t * TILE:(t + 1) * TILE, :] = part
            part = jnp.max(part.reshape(TILE // 8, 8, TILE), axis=0)
            part = jnp.where(allowed[abs(t - c)], part, -jnp.inf)
            largest = part if largest is None else jnp.maximum(largest, part)
        return jnp.max(largest, axis=0, keepdims=True)

    def second(s, c, block, allowed, largest, fresh):
        item = s * COLS + c
        before = jnp.where(fresh, -1e30, top[item, 0:1, :])
        row_top = jnp.maximum(before, largest)
        shift = row_top * SCALE2
        summed = jnp.where(fresh, 0.0, total[item]) * jnp.exp2((before - row_top) * SCALE2)
        for t in range(COLS):
            shift_here = jnp.where(allowed[abs(t - c)], shift, jnp.inf)
            weights = jnp.exp2(held[c, t * TILE:(t + 1) * TILE, :] * SCALE2 - shift_here).astype(BF16)
            values = jnp.concatenate([wide(kv_held[block, 1, t]), jnp.ones((16, TILE), BF16)], axis=0)
            summed = summed + jnp.dot(values, weights, preferred_element_type=F32)
        total[item] = summed
        top[item, 0:1, :] = row_top

    def gates(s, b):
        f, r = b // 3, lax.rem(b, 3)
        base = s * 5
        flag = jnp.where(f == 1, 1, jnp.where(f == 0, reach[base], reach[base + 1]))
        flag = flag * jnp.where(r == 1, 1, jnp.where(r == 0, reach[base + 2], reach[base + 3]))
        columns = jnp.where(flag > 0, reach[base + 4], -1)
        return [columns >= gap for gap in range(COLS)]

    def finish_last_column(s, b):
        second(s, COLS - 1, jnp.where(s == SLOTS, 4, s * 9 + b), gates(s, b), waiting[0:1, :], b == 4)

    def attend_block(s, b, s_before, b_before):
        allowed = gates(s, b)
        block = s * 9 + b
        largest = first(s, 0, block, allowed)
        finish_last_column(s_before, b_before)
        for c in range(COLS - 1):
            following = first(s, c + 1, block, allowed)
            second(s, c, block, allowed, largest, b == 4)
            largest = following
        waiting[0:1, :] = largest

    steps = timetable(layout)
    last_of = {s: i for i, (_, (s, _)) in enumerate(steps)}

    def pick(i, values):
        chosen = jnp.int32(values[0])
        for number, value in enumerate(values):
            if number and value != values[0]:
                chosen = jnp.where(i == number, value, chosen)
        return chosen

    def run_step(i, pending):
        for number, (waits, _) in enumerate(steps):
            if waits:
                @pl.when(i == number)
                def _(waits=waits):
                    for kind, s in waits:
                        wait(kind, s)
        s = pick(i, [job[0] for _, job in steps])
        b = pick(i, [job[1] for _, job in steps])
        f, r = b // 3, lax.rem(b, 3)
        inside = jnp.logical_and(
            jnp.logical_and(ftile + f >= 1, ftile + f <= FTILES), jnp.logical_and(row + r >= 1, row + r <= ROWS))

        @pl.when(inside)
        def _():
            attend_block(s, b, *pending)

        pending = tuple(jnp.where(inside, new, old) for new, old in zip((s, b), pending))
        done = pick(i, [int(last_of[job[0]] == number) for number, (_, job) in enumerate(steps)]) == 1

        @pl.when(done)
        def _():
            finish_last_column(*pending)
            for c in range(COLS):
                summed = total[s * COLS + c]
                blended = summed[:HEAD_DIM] / summed[HEAD_DIM:HEAD_DIM + 1]
                result[s * COLS + c] = jnp.transpose(blended).astype(BF16)
            o_keep(s).start()
            for step in lanes:
                o_copy(s, step).start()

        return jnp.where(done, SLOTS, pending[0]), jnp.where(done, 4, pending[1])

    lax.fori_loop(0, H, load_raw, 0)
    waiting[...] = jnp.zeros_like(waiting)
    held[COLS - 1] = jnp.zeros((COLS * TILE, TILE), F32)
    lax.fori_loop(0, H, wait_raw, 0)
    pack_slot(0)
    pl.semaphore_wait(barrier, peers)
    start_y(0)
    pack_slot(1)
    start_y(1)
    for s in range(2, SLOTS):
        pack_slot(s)
    lax.fori_loop(0, len(steps), run_step, (jnp.int32(SLOTS), jnp.int32(4)))

    for s, (has_frame, has_row) in enumerate(layout):
        o_keep(s).wait()
        for step in lanes:
            o_copy(s, step).wait()
            for copy in y_copies(s, step):
                copy.wait_send()
        for way in (1, -1):
            if has_frame:
                @pl.when(has[("z", way)])
                def _(s=s, way=way):
                    z_copy(s, way).wait_send()
            if has_row:
                for f in (0, 1, 2) if has_frame else (1,):
                    when_row(f, way, lambda s=s, f=f, way=way: x_copy(s, f, way).wait_send())


def fused(number, order, reach, queries, key_rows, value_rows):
    dma = pltpu.SemaphoreType.DMA
    smem = pl.BlockSpec(memory_space=pltpu.SMEM)
    any_space = pl.BlockSpec(memory_space=pl.ANY)
    items = SLOTS * COLS
    return pl.pallas_call(
        functools.partial(fused_kernel, LAYOUTS[number]),
        out_shape=jax.ShapeDtypeStruct((items, TILE, HEAD_DIM), BF16),
        in_specs=[smem, smem, any_space, any_space, any_space],
        out_specs=any_space,
        scratch_shapes=[
            pltpu.VMEM((3, H, TILE, HEAD_DIM), BF16),
            pltpu.VMEM((SLOTS, COLS, 3, TILE, HEAD_DIM), BF16),
            pltpu.VMEM((items, TILE, HEAD_DIM), BF16),
            pltpu.VMEM((SLOTS * 9, 2, COLS, TILE, HEAD_DIM), BF16),
            pltpu.VMEM((COLS, COLS * TILE, TILE), F32),
            pltpu.VMEM((items + COLS, HEAD_DIM + 16, TILE), F32),
            pltpu.VMEM((items + COLS, 8, TILE), F32),
            pltpu.VMEM((8, TILE), F32),
            pltpu.VMEM((items, TILE, HEAD_DIM), BF16),
            dma((3, H)),
            dma((SLOTS, 2)),
            dma((SLOTS, 3, 2)),
            dma((SLOTS, 3, 2)),
            dma((SLOTS, 2)),
            dma((SLOTS, 2)),
            dma((SLOTS, 3, 2)),
            dma((SLOTS, 3, 2)),
            dma((SLOTS,)),
            dma((SLOTS, 3)),
            dma((SLOTS, 3)),
        ],
        compiler_params=pltpu.CompilerParams(
            collective_id=number, has_side_effects=True, vmem_limit_bytes=60 * 2**20
        ),
        name="fused",
    )(order, reach, queries, key_rows, value_rows)


def place_kernel(order, back_ref, o_ref):
    def one(i, _):
        column = pl.ds(pl.multiple_of(order[i] * HEAD_DIM, HEAD_DIM), HEAD_DIM)
        o_ref[:, column] = back_ref[i]
        return 0
    lax.fori_loop(0, H, one, 0)


def place(order, back):
    return pl.pallas_call(
        place_kernel,
        out_shape=jax.ShapeDtypeStruct((TILE, H * HEAD_DIM), BF16),
        in_specs=[pl.BlockSpec(memory_space=pltpu.SMEM), pl.BlockSpec(memory_space=pltpu.VMEM)],
        out_specs=pl.BlockSpec(memory_space=pltpu.VMEM),
        name="place",
    )(order, back)


def per_device(queries, key_rows, value_rows, window_mask):
    order, reach, choice = make_plan(window_mask)
    back = lax.switch(
        choice[0], [functools.partial(fused, number) for number in range(len(LAYOUTS))],
        order, reach, queries, key_rows, value_rows,
    )
    return place(order, back)


def solution(mesh):
    return jax.shard_map(
        per_device,
        mesh=mesh,
        in_specs=(
            P(("frame", "head"), None),
            P(("frame", "head"), None),
            P(("frame", "head"), None),
            P(None, "frame", None),
        ),
        out_specs=P(("frame", "head"), None),
        check_vma=False,
    )
```

```python
import functools
import math

import jax
import jax.numpy as jnp
from jax import lax
from jax.experimental import pallas as pl
from jax.experimental.pallas import tpu as pltpu
from jax.sharding import PartitionSpec as P

H = 24
HEAD_DIM = 128
TILE = 256
COLS = 4
ROWS = 8
FTILES = 4
SLOTS = 6
SCALE2 = math.log2(math.e) / math.sqrt(HEAD_DIM)
F32 = jnp.float32
BF16 = jnp.bfloat16

LAYOUTS = (
    ((1, 1), (1, 1), (1, 0), (1, 0), (0, 1), (0, 0)),
    ((1, 1), (1, 1), (1, 0), (1, 0), (0, 1), (0, 1)),
    ((1, 1), (1, 1), (1, 1), (1, 0), (0, 1), (0, 0)),
    ((1, 1),) * 6,
)


def halves(tile):
    turned = jnp.transpose(tile)
    return jnp.concatenate([turned[:, :128], turned[:, 128:]], axis=0)


def plan_kernel(window, order, reach, choice, kinds, sizes, places):
    def measure(h, counts):
        sides = [window[h, 0, j] for j in (4, 28, 12, 20)]
        columns = window[h, 0, 17] + window[h, 0, 18] + window[h, 0, 19]
        for j, value in enumerate(sides + [columns]):
            sizes[h * 5 + j] = value
        frame = jnp.maximum(sides[0], sides[1])
        row = jnp.maximum(sides[2], sides[3])
        kind = jnp.where(frame > 0, 1 - row, 3 - row)
        kinds[h] = kind
        return tuple(whole + jnp.where(kind == k, 1, 0) for k, whole in enumerate(counts))

    many = lax.fori_loop(0, H, measure, (jnp.int32(0),) * 4, unroll=4)
    best = jnp.int32(len(LAYOUTS) - 1)
    for number in reversed(range(len(LAYOUTS) - 1)):
        layout = LAYOUTS[number]
        both = COLS * sum(f and r for f, r in layout)
        frames = COLS * sum(f for f, _ in layout)
        rows = COLS * sum(r and not f for f, r in layout)
        first_rows = many[0] + many[1] + many[2]
        fits = (many[0] <= both) & (many[0] + many[1] <= frames) & (first_rows <= frames + rows)
        fits = fits & ((many[2] == 0) | (many[0] + many[1] == frames))
        best = jnp.where(fits, number, best)
    choice[0] = best
    start = jnp.int32(0)
    for k in range(4):
        places[k] = start
        start = start + many[k]

    def deal(h, _):
        kind = kinds[h]
        place = places[kind]
        places[kind] = place + 1
        order[place] = h
        return 0

    lax.fori_loop(0, H, deal, 0, unroll=4)
    lane = lax.axis_index("head")
    for s in range(SLOTS):
        head = order[s * COLS + lane]
        for j in range(5):
            reach[s * 5 + j] = sizes[head * 5 + j]
    for j in range(5):
        reach[SLOTS * 5 + j] = 0


def make_plan(window_mask):
    smem = pl.BlockSpec(memory_space=pltpu.SMEM)
    return pl.pallas_call(
        plan_kernel,
        out_shape=(
            jax.ShapeDtypeStruct((H,), jnp.int32),
            jax.ShapeDtypeStruct((SLOTS * 5 + 5,), jnp.int32),
            jax.ShapeDtypeStruct((1,), jnp.int32),
        ),
        in_specs=[smem],
        out_specs=(smem, smem, smem),
        scratch_shapes=[
            pltpu.SMEM((H,), jnp.int32),
            pltpu.SMEM((H * 5,), jnp.int32),
            pltpu.SMEM((4,), jnp.int32),
        ],
        name="plan",
    )(window_mask)


def timetable(layout):
    y_time, z_time, x_time, block_time, end_time = 9.0, 13.0, 7.0, 1.3, 0.8
    events, z_free, x_ready = [], 0.0, []
    for s, (has_frame, has_row) in enumerate(layout):
        y_done = y_time * (s + 1) + 1
        events.append((y_done, ("y", s), ((s, 4),)))
        if has_frame:
            z_free = max(z_free, y_done) + z_time
            events.append((z_free, ("z", s), ((s, 1), (s, 7))))
        if has_row:
            x_ready.append((y_done, ("xc", s), ((s, 3), (s, 5)), x_time))
            if has_frame:
                x_ready.append((z_free, ("xk", s), ((s, 0), (s, 2), (s, 6), (s, 8)), 2 * x_time))
    x_free = 0.0
    for ready, name, jobs, length in sorted(x_ready):
        x_free = max(x_free, ready) + length
        events.append((x_free, name, jobs))
    events.sort()
    steps, waits, open_jobs, now = [], [], [], 0.0
    while events or open_jobs:
        while events and (events[0][0] <= now or not open_jobs):
            at, name, jobs = events.pop(0)
            now = max(now, at)
            waits.append(name)
            open_jobs.extend(jobs)
        open_jobs.sort(key=lambda job: (job[0], job[1] != 4))
        job = open_jobs.pop(0)
        steps.append((tuple(waits), job))
        waits = []
        now += block_time
        if not any(later[0] == job[0] for _, _, jobs in events for later in jobs) and not any(
                later[0] == job[0] for later in open_jobs):
            now += end_time
    return steps


def fused_kernel(
    layout, order, reach, q_in, k_in, v_in, back, raw, pack, q_held, kv_held, held, total, top, waiting, result,
    raw_sem, own_sem, y_send, y_recv, z_send, z_recv, x_send, x_recv, o_own, o_send, o_recv,
):
    frame = lax.axis_index("frame")
    lane = lax.axis_index("head")
    ftile, row = frame // ROWS, lax.rem(frame, ROWS)
    has = {
        ("z", 1): ftile < FTILES - 1,
        ("z", -1): ftile > 0,
        ("x", 1): row < ROWS - 1,
        ("x", -1): row > 0,
    }
    hop = {"z": ROWS, "x": 1}
    mesh_ids = pl.DeviceIdType.MESH
    lanes = (1, 3, 2)

    def at(axis, way):
        return {"frame": frame + way * hop[axis], "head": lane}

    def across(step):
        return {"frame": frame, "head": lax.rem(lane + step, COLS)}

    barrier = pltpu.get_barrier_semaphore()
    for step in lanes:
        pl.semaphore_signal(barrier, inc=1, device_id=across(step), device_id_type=mesh_ids)
    peers = jnp.int32(3)
    for (axis, way), there in has.items():
        peers = peers + jnp.where(there, 1, 0)

        @pl.when(there)
        def _(axis=axis, way=way):
            pl.semaphore_signal(barrier, inc=1, device_id=at(axis, way), device_id_type=mesh_ids)

    def raw_copies(h):
        column = pl.ds(pl.multiple_of(h * HEAD_DIM, HEAD_DIM), HEAD_DIM)
        return [
            pltpu.make_async_copy(source.at[:, column], raw.at[i, h], raw_sem.at[i, h])
            for i, source in enumerate((q_in, k_in, v_in))
        ]

    def load_raw(h, _):
        for copy in raw_copies(h):
            copy.start()
        return 0

    def wait_raw(h, _):
        for copy in raw_copies(h):
            copy.wait()
        return 0

    def pack_slot(s):
        def one(y, _):
            head = order[s * COLS + y]
            pack[s, y, 0] = halves(raw[0, head])
            pack[s, y, 1] = raw[1, head]
            pack[s, y, 2] = halves(raw[2, head])
            return 0

        lax.fori_loop(0, COLS, one, 0)

    def own_copies(s):
        return (
            pltpu.make_async_copy(pack.at[s, lane, 0], q_held.at[s * COLS + lane], own_sem.at[s, 0]),
            pltpu.make_async_copy(pack.at[s, lane, pl.ds(1, 2)], kv_held.at[s * 9 + 4, :, lane], own_sem.at[s, 1]),
        )

    def y_copies(s, step):
        peer = lax.rem(lane + step, COLS)
        return (
            pltpu.make_async_remote_copy(
                src_ref=pack.at[s, peer, pl.ds(1, 2)], dst_ref=kv_held.at[s * 9 + 4, :, lane],
                send_sem=y_send.at[s, step - 1, 1], recv_sem=y_recv.at[s, step - 1, 1],
                device_id=across(step), device_id_type=mesh_ids),
            pltpu.make_async_remote_copy(
                src_ref=pack.at[s, peer, 0], dst_ref=q_held.at[s * COLS + lane],
                send_sem=y_send.at[s, step - 1, 0], recv_sem=y_recv.at[s, step - 1, 0],
                device_id=across(step), device_id_type=mesh_ids),
        )

    def z_copy(s, way):
        side = 0 if way == 1 else 1
        return pltpu.make_async_remote_copy(
            src_ref=kv_held.at[s * 9 + 4], dst_ref=kv_held.at[s * 9 + (1 - way) * 3 + 1],
            send_sem=z_send.at[s, side], recv_sem=z_recv.at[s, side],
            device_id=at("z", way), device_id_type=mesh_ids)

    def x_copy(s, f, way):
        side = 0 if way == 1 else 1
        return pltpu.make_async_remote_copy(
            src_ref=kv_held.at[s * 9 + f * 3 + 1], dst_ref=kv_held.at[s * 9 + f * 3 + 1 - way],
            send_sem=x_send.at[s, f, side], recv_sem=x_recv.at[s, f, side],
            device_id=at("x", way), device_id_type=mesh_ids)

    def o_copy(s, step):
        peer = lax.rem(lane + step, COLS)
        return pltpu.make_async_remote_copy(
            src_ref=result.at[s * COLS + peer], dst_ref=back.at[s * COLS + lane],
            send_sem=o_send.at[s, step - 1], recv_sem=o_recv.at[s, step - 1],
            device_id=across(step), device_id_type=mesh_ids)

    def o_keep(s):
        return pltpu.make_async_copy(result.at[s * COLS + lane], back.at[s * COLS + lane], o_own.at[s])

    def present(f):
        return True if f == 1 else has[("z", -1 if f == 0 else 1)]

    def when_row(f, way, act):
        @pl.when(jnp.logical_and(has[("x", way)], present(f)))
        def _():
            act()

    def start_y(s):
        for copy in own_copies(s):
            copy.start()
        for step in lanes:
            for copy in y_copies(s, step):
                copy.start()

    def wait(kind, s):
        has_frame, has_row = layout[s]
        if kind == "y":
            for copy in own_copies(s):
                copy.wait()
            for step in lanes:
                for copy in y_copies(s, step):
                    copy.wait_recv()
            if s + 2 < SLOTS:
                start_y(s + 2)
            for way in (1, -1):
                if has_frame:
                    @pl.when(has[("z", way)])
                    def _(way=way):
                        z_copy(s, way).start()
                if has_row:
                    when_row(1, way, lambda way=way: x_copy(s, 1, way).start())
        elif kind == "z":
            for way in (1, -1):
                @pl.when(has[("z", -way)])
                def _(way=way):
                    z_copy(s, way).wait_recv()
            if has_row:
                for f in (0, 2):
                    for way in (1, -1):
                        when_row(f, way, lambda f=f, way=way: x_copy(s, f, way).start())
        else:
            for f in (1,) if kind == "xc" else (0, 2):
                for way in (1, -1):
                    when_row(f, -way, lambda f=f, way=way: x_copy(s, f, way).wait_recv())

    def wide(tile):
        return jnp.concatenate([tile[:128], tile[128:]], axis=1)

    def first(s, c, block, allowed):
        q_turned = wide(q_held[s * COLS + c])
        largest = None
        for t in range(COLS):
            part = jnp.dot(kv_held[block, 0, t], q_turned, preferred_element_type=F32)
            held[c, t * TILE:(t + 1) * TILE, :] = part
            part = jnp.max(part.reshape(TILE // 8, 8, TILE), axis=0)
            part = jnp.where(allowed[abs(t - c)], part, -jnp.inf)
            largest = part if largest is None else jnp.maximum(largest, part)
        return jnp.max(largest, axis=0, keepdims=True)

    def second(s, c, block, allowed, largest, fresh):
        item = s * COLS + c
        before = jnp.where(fresh, -1e30, top[item, 0:1, :])
        row_top = jnp.maximum(before, largest)
        shift = row_top * SCALE2
        summed = jnp.where(fresh, 0.0, total[item]) * jnp.exp2((before - row_top) * SCALE2)
        for t in range(COLS):
            shift_here = jnp.where(allowed[abs(t - c)], shift, jnp.inf)
            weights = jnp.exp2(held[c, t * TILE:(t + 1) * TILE, :] * SCALE2 - shift_here).astype(BF16)
            values = jnp.concatenate([wide(kv_held[block, 1, t]), jnp.ones((16, TILE), BF16)], axis=0)
            summed = summed + jnp.dot(values, weights, preferred_element_type=F32)
        total[item] = summed
        top[item, 0:1, :] = row_top

    def gates(s, b):
        f, r = b // 3, lax.rem(b, 3)
        base = s * 5
        flag = jnp.where(f == 1, 1, jnp.where(f == 0, reach[base], reach[base + 1]))
        flag = flag * jnp.where(r == 1, 1, jnp.where(r == 0, reach[base + 2], reach[base + 3]))
        columns = jnp.where(flag > 0, reach[base + 4], -1)
        return [columns >= gap for gap in range(COLS)]

    def finish_last_column(s, b):
        second(s, COLS - 1, jnp.where(s == SLOTS, 4, s * 9 + b), gates(s, b), waiting[0:1, :], b == 4)

    def attend_block(s, b, s_before, b_before):
        allowed = gates(s, b)
        block = s * 9 + b
        largest = first(s, 0, block, allowed)
        finish_last_column(s_before, b_before)
        for c in range(COLS - 1):
            following = first(s, c + 1, block, allowed)
            second(s, c, block, allowed, largest, b == 4)
            largest = following
        waiting[0:1, :] = largest

    steps = timetable(layout)
    last_of = {s: i for i, (_, (s, _)) in enumerate(steps)}

    def pick(i, values):
        chosen = jnp.int32(values[0])
        for number, value in enumerate(values):
            if number and value != values[0]:
                chosen = jnp.where(i == number, value, chosen)
        return chosen

    def run_step(i, pending):
        for number, (waits, _) in enumerate(steps):
            if waits:
                @pl.when(i == number)
                def _(waits=waits):
                    for kind, s in waits:
                        wait(kind, s)
        s = pick(i, [job[0] for _, job in steps])
        b = pick(i, [job[1] for _, job in steps])
        f, r = b // 3, lax.rem(b, 3)
        inside = jnp.logical_and(
            jnp.logical_and(ftile + f >= 1, ftile + f <= FTILES), jnp.logical_and(row + r >= 1, row + r <= ROWS))

        @pl.when(inside)
        def _():
            attend_block(s, b, *pending)

        pending = tuple(jnp.where(inside, new, old) for new, old in zip((s, b), pending))
        done = pick(i, [int(last_of[job[0]] == number) for number, (_, job) in enumerate(steps)]) == 1

        @pl.when(done)
        def _():
            finish_last_column(*pending)
            for c in range(COLS):
                summed = total[s * COLS + c]
                blended = summed[:HEAD_DIM] / summed[HEAD_DIM:HEAD_DIM + 1]
                result[s * COLS + c] = jnp.transpose(blended).astype(BF16)
            o_keep(s).start()
            for step in lanes:
                o_copy(s, step).start()

        return jnp.where(done, SLOTS, pending[0]), jnp.where(done, 4, pending[1])

    lax.fori_loop(0, H, load_raw, 0)
    waiting[...] = jnp.zeros_like(waiting)
    held[COLS - 1] = jnp.zeros((COLS * TILE, TILE), F32)
    lax.fori_loop(0, H, wait_raw, 0)
    pack_slot(0)
    pl.semaphore_wait(barrier, peers)
    start_y(0)
    pack_slot(1)
    start_y(1)
    for s in range(2, SLOTS):
        pack_slot(s)
    lax.fori_loop(0, len(steps), run_step, (jnp.int32(SLOTS), jnp.int32(4)))

    for s, (has_frame, has_row) in enumerate(layout):
        o_keep(s).wait()
        for step in lanes:
            o_copy(s, step).wait()
            for copy in y_copies(s, step):
                copy.wait_send()
        for way in (1, -1):
            if has_frame:
                @pl.when(has[("z", way)])
                def _(s=s, way=way):
                    z_copy(s, way).wait_send()
            if has_row:
                for f in (0, 1, 2) if has_frame else (1,):
                    when_row(f, way, lambda s=s, f=f, way=way: x_copy(s, f, way).wait_send())


def fused(number, order, reach, queries, key_rows, value_rows):
    dma = pltpu.SemaphoreType.DMA
    smem = pl.BlockSpec(memory_space=pltpu.SMEM)
    any_space = pl.BlockSpec(memory_space=pl.ANY)
    items = SLOTS * COLS
    return pl.pallas_call(
        functools.partial(fused_kernel, LAYOUTS[number]),
        out_shape=jax.ShapeDtypeStruct((items, TILE, HEAD_DIM), BF16),
        in_specs=[smem, smem, any_space, any_space, any_space],
        out_specs=any_space,
        scratch_shapes=[
            pltpu.VMEM((3, H, TILE, HEAD_DIM), BF16),
            pltpu.VMEM((SLOTS, COLS, 3, TILE, HEAD_DIM), BF16),
            pltpu.VMEM((items, TILE, HEAD_DIM), BF16),
            pltpu.VMEM((SLOTS * 9, 2, COLS, TILE, HEAD_DIM), BF16),
            pltpu.VMEM((COLS, COLS * TILE, TILE), F32),
            pltpu.VMEM((items + COLS, HEAD_DIM + 16, TILE), F32),
            pltpu.VMEM((items + COLS, 8, TILE), F32),
            pltpu.VMEM((8, TILE), F32),
            pltpu.VMEM((items, TILE, HEAD_DIM), BF16),
            dma((3, H)),
            dma((SLOTS, 2)),
            dma((SLOTS, 3, 2)),
            dma((SLOTS, 3, 2)),
            dma((SLOTS, 2)),
            dma((SLOTS, 2)),
            dma((SLOTS, 3, 2)),
            dma((SLOTS, 3, 2)),
            dma((SLOTS,)),
            dma((SLOTS, 3)),
            dma((SLOTS, 3)),
        ],
        compiler_params=pltpu.CompilerParams(
            collective_id=number, has_side_effects=True, vmem_limit_bytes=60 * 2**20
        ),
        name="fused",
    )(order, reach, queries, key_rows, value_rows)


def place_kernel(order, back_ref, o_ref):
    def one(i, _):
        column = pl.ds(pl.multiple_of(order[i] * HEAD_DIM, HEAD_DIM), HEAD_DIM)
        o_ref[:, column] = back_ref[i]
        return 0
    lax.fori_loop(0, H, one, 0)


def place(order, back):
    return pl.pallas_call(
        place_kernel,
        out_shape=jax.ShapeDtypeStruct((TILE, H * HEAD_DIM), BF16),
        in_specs=[pl.BlockSpec(memory_space=pltpu.SMEM), pl.BlockSpec(memory_space=pltpu.VMEM)],
        out_specs=pl.BlockSpec(memory_space=pltpu.VMEM),
        name="place",
    )(order, back)


def per_device(queries, key_rows, value_rows, window_mask):
    order, reach, choice = make_plan(window_mask)
    back = lax.switch(
        choice[0], [functools.partial(fused, number) for number in range(len(LAYOUTS))],
        order, reach, queries, key_rows, value_rows,
    )
    return place(order, back)


def solution(mesh):
    return jax.shard_map(
        per_device,
        mesh=mesh,
        in_specs=(
            P(("frame", "head"), None),
            P(("frame", "head"), None),
            P(("frame", "head"), None),
            P(None, "frame", None),
        ),
        out_specs=P(("frame", "head"), None),
        check_vma=False,
    )
```

```python
import functools
import math

import jax
import jax.numpy as jnp
from jax import lax
from jax.experimental import pallas as pl
from jax.experimental.pallas import tpu as pltpu
from jax.sharding import PartitionSpec as P

H = 24
HEAD_DIM = 128
TILE = 256
COLS = 4
ROWS = 8
FTILES = 4
SLOTS = 6
SCALE2 = math.log2(math.e) / math.sqrt(HEAD_DIM)
F32 = jnp.float32
BF16 = jnp.bfloat16

LAYOUTS = (
    ((1, 1), (1, 1), (1, 0), (1, 0), (0, 1), (0, 0)),
    ((1, 1), (1, 1), (1, 0), (1, 0), (0, 1), (0, 1)),
    ((1, 1), (1, 1), (1, 1), (1, 0), (0, 1), (0, 0)),
    ((1, 1),) * 6,
)


def halves(tile):
    turned = jnp.transpose(tile)
    return jnp.concatenate([turned[:, :128], turned[:, 128:]], axis=0)


def plan_kernel(window, order, reach, choice, kinds, sizes, places):
    def measure(h, counts):
        sides = [window[h, 0, j] for j in (4, 28, 12, 20)]
        columns = window[h, 0, 17] + window[h, 0, 18] + window[h, 0, 19]
        for j, value in enumerate(sides + [columns]):
            sizes[h * 5 + j] = value
        frame = jnp.maximum(sides[0], sides[1])
        row = jnp.maximum(sides[2], sides[3])
        kind = jnp.where(frame > 0, 1 - row, 3 - row)
        kinds[h] = kind
        return tuple(whole + jnp.where(kind == k, 1, 0) for k, whole in enumerate(counts))

    many = lax.fori_loop(0, H, measure, (jnp.int32(0),) * 4, unroll=4)
    best = jnp.int32(len(LAYOUTS) - 1)
    for number in reversed(range(len(LAYOUTS) - 1)):
        layout = LAYOUTS[number]
        both = COLS * sum(f and r for f, r in layout)
        frames = COLS * sum(f for f, _ in layout)
        rows = COLS * sum(r and not f for f, r in layout)
        first_rows = many[0] + many[1] + many[2]
        fits = (many[0] <= both) & (many[0] + many[1] <= frames) & (first_rows <= frames + rows)
        fits = fits & ((many[2] == 0) | (many[0] + many[1] == frames))
        best = jnp.where(fits, number, best)
    choice[0] = best
    start = jnp.int32(0)
    for k in range(4):
        places[k] = start
        start = start + many[k]

    def deal(h, _):
        kind = kinds[h]
        place = places[kind]
        places[kind] = place + 1
        order[place] = h
        return 0

    lax.fori_loop(0, H, deal, 0, unroll=4)
    lane = lax.axis_index("head")
    for s in range(SLOTS):
        head = order[s * COLS + lane]
        for j in range(5):
            reach[s * 5 + j] = sizes[head * 5 + j]
    for j in range(5):
        reach[SLOTS * 5 + j] = 0


def make_plan(window_mask):
    smem = pl.BlockSpec(memory_space=pltpu.SMEM)
    return pl.pallas_call(
        plan_kernel,
        out_shape=(
            jax.ShapeDtypeStruct((H,), jnp.int32),
            jax.ShapeDtypeStruct((SLOTS * 5 + 5,), jnp.int32),
            jax.ShapeDtypeStruct((1,), jnp.int32),
        ),
        in_specs=[smem],
        out_specs=(smem, smem, smem),
        scratch_shapes=[
            pltpu.SMEM((H,), jnp.int32),
            pltpu.SMEM((H * 5,), jnp.int32),
            pltpu.SMEM((4,), jnp.int32),
        ],
        name="plan",
    )(window_mask)


def timetable(layout):
    wide_rows = sum(frame and row for frame, row in layout) == 3
    y_time, z_time, x_time = (9.5, 12.0, 6.5) if wide_rows else (9.0, 13.0, 7.0)
    block_time, end_time = 1.3, 0.8
    events, z_free, x_ready = [], 0.0, []
    for s, (has_frame, has_row) in enumerate(layout):
        y_done = y_time * (s + 1) + 1
        events.append((y_done, ("y", s), ((s, 4),)))
        if has_frame:
            z_free = max(z_free, y_done) + z_time
            events.append((z_free, ("z", s), ((s, 1), (s, 7))))
        if has_row:
            x_ready.append((y_done, ("xc", s), ((s, 3), (s, 5)), x_time))
            if has_frame:
                x_ready.append((z_free, ("xk", s), ((s, 0), (s, 2), (s, 6), (s, 8)), 2 * x_time))
    x_free = 0.0
    for ready, name, jobs, length in sorted(x_ready):
        x_free = max(x_free, ready) + length
        events.append((x_free, name, jobs))
    events.sort()
    steps, waits, open_jobs, now = [], [], [], 0.0
    while events or open_jobs:
        while events and (events[0][0] <= now or not open_jobs):
            at, name, jobs = events.pop(0)
            now = max(now, at)
            waits.append(name)
            open_jobs.extend(jobs)
        open_jobs.sort(key=lambda job: (-job[0] if wide_rows else job[0], job[1] != 4))
        job = open_jobs.pop(0)
        steps.append((tuple(waits), job))
        waits = []
        now += block_time
        if not any(later[0] == job[0] for _, _, jobs in events for later in jobs) and not any(
                later[0] == job[0] for later in open_jobs):
            now += end_time
    return steps


def fused_kernel(
    layout, order, reach, q_in, k_in, v_in, back, raw, pack, q_held, kv_held, held, total, top, waiting, result,
    raw_sem, own_sem, y_send, y_recv, z_send, z_recv, x_send, x_recv, o_own, o_send, o_recv,
):
    frame = lax.axis_index("frame")
    lane = lax.axis_index("head")
    ftile, row = frame // ROWS, lax.rem(frame, ROWS)
    has = {
        ("z", 1): ftile < FTILES - 1,
        ("z", -1): ftile > 0,
        ("x", 1): row < ROWS - 1,
        ("x", -1): row > 0,
    }
    hop = {"z": ROWS, "x": 1}
    mesh_ids = pl.DeviceIdType.MESH
    lanes = (1, 3, 2)

    def at(axis, way):
        return {"frame": frame + way * hop[axis], "head": lane}

    def across(step):
        return {"frame": frame, "head": lax.rem(lane + step, COLS)}

    barrier = pltpu.get_barrier_semaphore()
    for step in lanes:
        pl.semaphore_signal(barrier, inc=1, device_id=across(step), device_id_type=mesh_ids)
    peers = jnp.int32(3)
    for (axis, way), there in has.items():
        peers = peers + jnp.where(there, 1, 0)

        @pl.when(there)
        def _(axis=axis, way=way):
            pl.semaphore_signal(barrier, inc=1, device_id=at(axis, way), device_id_type=mesh_ids)

    def raw_copies(h):
        column = pl.ds(pl.multiple_of(h * HEAD_DIM, HEAD_DIM), HEAD_DIM)
        return [
            pltpu.make_async_copy(source.at[:, column], raw.at[i, h], raw_sem.at[i, h])
            for i, source in enumerate((q_in, k_in, v_in))
        ]

    def load_raw(h, _):
        for copy in raw_copies(h):
            copy.start()
        return 0

    def wait_raw(h, _):
        for copy in raw_copies(h):
            copy.wait()
        return 0

    def pack_slot(s):
        def one(y, _):
            head = order[s * COLS + y]
            pack[s, y, 0] = halves(raw[0, head])
            pack[s, y, 1] = raw[1, head]
            pack[s, y, 2] = halves(raw[2, head])
            return 0

        lax.fori_loop(0, COLS, one, 0)

    def own_copies(s):
        return (
            pltpu.make_async_copy(pack.at[s, lane, 0], q_held.at[s * COLS + lane], own_sem.at[s, 0]),
            pltpu.make_async_copy(pack.at[s, lane, pl.ds(1, 2)], kv_held.at[s * 9 + 4, :, lane], own_sem.at[s, 1]),
        )

    def y_copies(s, step):
        peer = lax.rem(lane + step, COLS)
        return (
            pltpu.make_async_remote_copy(
                src_ref=pack.at[s, peer, pl.ds(1, 2)], dst_ref=kv_held.at[s * 9 + 4, :, lane],
                send_sem=y_send.at[s, step - 1, 1], recv_sem=y_recv.at[s, step - 1, 1],
                device_id=across(step), device_id_type=mesh_ids),
            pltpu.make_async_remote_copy(
                src_ref=pack.at[s, peer, 0], dst_ref=q_held.at[s * COLS + lane],
                send_sem=y_send.at[s, step - 1, 0], recv_sem=y_recv.at[s, step - 1, 0],
                device_id=across(step), device_id_type=mesh_ids),
        )

    def z_copy(s, way):
        side = 0 if way == 1 else 1
        return pltpu.make_async_remote_copy(
            src_ref=kv_held.at[s * 9 + 4], dst_ref=kv_held.at[s * 9 + (1 - way) * 3 + 1],
            send_sem=z_send.at[s, side], recv_sem=z_recv.at[s, side],
            device_id=at("z", way), device_id_type=mesh_ids)

    def x_copy(s, f, way):
        side = 0 if way == 1 else 1
        return pltpu.make_async_remote_copy(
            src_ref=kv_held.at[s * 9 + f * 3 + 1], dst_ref=kv_held.at[s * 9 + f * 3 + 1 - way],
            send_sem=x_send.at[s, f, side], recv_sem=x_recv.at[s, f, side],
            device_id=at("x", way), device_id_type=mesh_ids)

    def o_copy(s, step):
        peer = lax.rem(lane + step, COLS)
        return pltpu.make_async_remote_copy(
            src_ref=result.at[s * COLS + peer], dst_ref=back.at[s * COLS + lane],
            send_sem=o_send.at[s, step - 1], recv_sem=o_recv.at[s, step - 1],
            device_id=across(step), device_id_type=mesh_ids)

    def o_keep(s):
        return pltpu.make_async_copy(result.at[s * COLS + lane], back.at[s * COLS + lane], o_own.at[s])

    def present(f):
        return True if f == 1 else has[("z", -1 if f == 0 else 1)]

    def when_row(f, way, act):
        @pl.when(jnp.logical_and(has[("x", way)], present(f)))
        def _():
            act()

    def start_y(s):
        for copy in own_copies(s):
            copy.start()
        for step in lanes:
            for copy in y_copies(s, step):
                copy.start()

    def wait(kind, s):
        has_frame, has_row = layout[s]
        if kind == "y":
            for copy in own_copies(s):
                copy.wait()
            for step in lanes:
                for copy in y_copies(s, step):
                    copy.wait_recv()
            if s + 2 < SLOTS:
                start_y(s + 2)
            for way in (1, -1):
                if has_frame:
                    @pl.when(has[("z", way)])
                    def _(way=way):
                        z_copy(s, way).start()
                if has_row:
                    when_row(1, way, lambda way=way: x_copy(s, 1, way).start())
        elif kind == "z":
            for way in (1, -1):
                @pl.when(has[("z", -way)])
                def _(way=way):
                    z_copy(s, way).wait_recv()
            if has_row:
                for f in (0, 2):
                    for way in (1, -1):
                        when_row(f, way, lambda f=f, way=way: x_copy(s, f, way).start())
        else:
            for f in (1,) if kind == "xc" else (0, 2):
                for way in (1, -1):
                    when_row(f, -way, lambda f=f, way=way: x_copy(s, f, way).wait_recv())

    def wide(tile):
        return jnp.concatenate([tile[:128], tile[128:]], axis=1)

    def first(s, c, block, allowed):
        q_turned = wide(q_held[s * COLS + c])
        largest = None
        for t in range(COLS):
            part = jnp.dot(kv_held[block, 0, t], q_turned, preferred_element_type=F32)
            held[c, t * TILE:(t + 1) * TILE, :] = part
            part = jnp.max(part.reshape(TILE // 8, 8, TILE), axis=0)
            part = jnp.where(allowed[abs(t - c)], part, -jnp.inf)
            largest = part if largest is None else jnp.maximum(largest, part)
        return jnp.max(largest, axis=0, keepdims=True)

    def second(s, c, block, allowed, largest, fresh):
        item = s * COLS + c
        before = jnp.where(fresh, -1e30, top[item, 0:1, :])
        row_top = jnp.maximum(before, largest)
        shift = row_top * SCALE2
        summed = jnp.where(fresh, 0.0, total[item]) * jnp.exp2((before - row_top) * SCALE2)
        for t in range(COLS):
            shift_here = jnp.where(allowed[abs(t - c)], shift, jnp.inf)
            weights = jnp.exp2(held[c, t * TILE:(t + 1) * TILE, :] * SCALE2 - shift_here).astype(BF16)
            values = jnp.concatenate([wide(kv_held[block, 1, t]), jnp.ones((16, TILE), BF16)], axis=0)
            summed = summed + jnp.dot(values, weights, preferred_element_type=F32)
        total[item] = summed
        top[item, 0:1, :] = row_top

    def gates(s, b):
        f, r = b // 3, lax.rem(b, 3)
        base = s * 5
        flag = jnp.where(f == 1, 1, jnp.where(f == 0, reach[base], reach[base + 1]))
        flag = flag * jnp.where(r == 1, 1, jnp.where(r == 0, reach[base + 2], reach[base + 3]))
        columns = jnp.where(flag > 0, reach[base + 4], -1)
        return [columns >= gap for gap in range(COLS)]

    def finish_last_column(s, b):
        second(s, COLS - 1, jnp.where(s == SLOTS, 4, s * 9 + b), gates(s, b), waiting[0:1, :], b == 4)

    def attend_block(s, b, s_before, b_before):
        allowed = gates(s, b)
        block = s * 9 + b
        largest = first(s, 0, block, allowed)
        finish_last_column(s_before, b_before)
        for c in range(COLS - 1):
            following = first(s, c + 1, block, allowed)
            second(s, c, block, allowed, largest, b == 4)
            largest = following
        waiting[0:1, :] = largest

    steps = timetable(layout)
    last_of = {s: i for i, (_, (s, _)) in enumerate(steps)}

    def pick(i, values):
        chosen = jnp.int32(values[0])
        for number, value in enumerate(values):
            if number and value != values[0]:
                chosen = jnp.where(i == number, value, chosen)
        return chosen

    def run_step(i, pending):
        for number, (waits, _) in enumerate(steps):
            if waits:
                @pl.when(i == number)
                def _(waits=waits):
                    for kind, s in waits:
                        wait(kind, s)
        s = pick(i, [job[0] for _, job in steps])
        b = pick(i, [job[1] for _, job in steps])
        f, r = b // 3, lax.rem(b, 3)
        inside = jnp.logical_and(
            jnp.logical_and(ftile + f >= 1, ftile + f <= FTILES), jnp.logical_and(row + r >= 1, row + r <= ROWS))

        @pl.when(inside)
        def _():
            attend_block(s, b, *pending)

        pending = tuple(jnp.where(inside, new, old) for new, old in zip((s, b), pending))
        done = pick(i, [int(last_of[job[0]] == number) for number, (_, job) in enumerate(steps)]) == 1

        @pl.when(done)
        def _():
            finish_last_column(*pending)
            for c in range(COLS):
                summed = total[s * COLS + c]
                blended = summed[:HEAD_DIM] / summed[HEAD_DIM:HEAD_DIM + 1]
                result[s * COLS + c] = jnp.transpose(blended).astype(BF16)
            o_keep(s).start()
            for step in lanes:
                o_copy(s, step).start()

        return jnp.where(done, SLOTS, pending[0]), jnp.where(done, 4, pending[1])

    lax.fori_loop(0, H, load_raw, 0)
    waiting[...] = jnp.zeros_like(waiting)
    held[COLS - 1] = jnp.zeros((COLS * TILE, TILE), F32)
    lax.fori_loop(0, H, wait_raw, 0)
    pack_slot(0)
    pl.semaphore_wait(barrier, peers)
    start_y(0)
    pack_slot(1)
    start_y(1)
    for s in range(2, SLOTS):
        pack_slot(s)
    lax.fori_loop(0, len(steps), run_step, (jnp.int32(SLOTS), jnp.int32(4)))

    for s, (has_frame, has_row) in enumerate(layout):
        o_keep(s).wait()
        for step in lanes:
            o_copy(s, step).wait()
            for copy in y_copies(s, step):
                copy.wait_send()
        for way in (1, -1):
            if has_frame:
                @pl.when(has[("z", way)])
                def _(s=s, way=way):
                    z_copy(s, way).wait_send()
            if has_row:
                for f in (0, 1, 2) if has_frame else (1,):
                    when_row(f, way, lambda s=s, f=f, way=way: x_copy(s, f, way).wait_send())


def fused(number, order, reach, queries, key_rows, value_rows):
    dma = pltpu.SemaphoreType.DMA
    smem = pl.BlockSpec(memory_space=pltpu.SMEM)
    any_space = pl.BlockSpec(memory_space=pl.ANY)
    items = SLOTS * COLS
    return pl.pallas_call(
        functools.partial(fused_kernel, LAYOUTS[number]),
        out_shape=jax.ShapeDtypeStruct((items, TILE, HEAD_DIM), BF16),
        in_specs=[smem, smem, any_space, any_space, any_space],
        out_specs=any_space,
        scratch_shapes=[
            pltpu.VMEM((3, H, TILE, HEAD_DIM), BF16),
            pltpu.VMEM((SLOTS, COLS, 3, TILE, HEAD_DIM), BF16),
            pltpu.VMEM((items, TILE, HEAD_DIM), BF16),
            pltpu.VMEM((SLOTS * 9, 2, COLS, TILE, HEAD_DIM), BF16),
            pltpu.VMEM((COLS, COLS * TILE, TILE), F32),
            pltpu.VMEM((items + COLS, HEAD_DIM + 16, TILE), F32),
            pltpu.VMEM((items + COLS, 8, TILE), F32),
            pltpu.VMEM((8, TILE), F32),
            pltpu.VMEM((items, TILE, HEAD_DIM), BF16),
            dma((3, H)),
            dma((SLOTS, 2)),
            dma((SLOTS, 3, 2)),
            dma((SLOTS, 3, 2)),
            dma((SLOTS, 2)),
            dma((SLOTS, 2)),
            dma((SLOTS, 3, 2)),
            dma((SLOTS, 3, 2)),
            dma((SLOTS,)),
            dma((SLOTS, 3)),
            dma((SLOTS, 3)),
        ],
        compiler_params=pltpu.CompilerParams(
            collective_id=number, has_side_effects=True, vmem_limit_bytes=60 * 2**20
        ),
        name="fused",
    )(order, reach, queries, key_rows, value_rows)


def place_kernel(order, back_ref, o_ref):
    def one(i, _):
        column = pl.ds(pl.multiple_of(order[i] * HEAD_DIM, HEAD_DIM), HEAD_DIM)
        o_ref[:, column] = back_ref[i]
        return 0
    lax.fori_loop(0, H, one, 0)


def place(order, back):
    return pl.pallas_call(
        place_kernel,
        out_shape=jax.ShapeDtypeStruct((TILE, H * HEAD_DIM), BF16),
        in_specs=[pl.BlockSpec(memory_space=pltpu.SMEM), pl.BlockSpec(memory_space=pltpu.VMEM)],
        out_specs=pl.BlockSpec(memory_space=pltpu.VMEM),
        name="place",
    )(order, back)


def per_device(queries, key_rows, value_rows, window_mask):
    order, reach, choice = make_plan(window_mask)
    back = lax.switch(
        choice[0], [functools.partial(fused, number) for number in range(len(LAYOUTS))],
        order, reach, queries, key_rows, value_rows,
    )
    return place(order, back)


def solution(mesh):
    return jax.shard_map(
        per_device,
        mesh=mesh,
        in_specs=(
            P(("frame", "head"), None),
            P(("frame", "head"), None),
            P(("frame", "head"), None),
            P(None, "frame", None),
        ),
        out_specs=P(("frame", "head"), None),
        check_vma=False,
    )
```

```python
import functools
import math

import jax
import jax.numpy as jnp
from jax import lax
from jax.experimental import pallas as pl
from jax.experimental.pallas import tpu as pltpu
from jax.sharding import PartitionSpec as P

H = 24
HEAD_DIM = 128
TILE = 256
COLS = 4
ROWS = 8
FTILES = 4
SLOTS = 6
SCALE2 = math.log2(math.e) / math.sqrt(HEAD_DIM)
F32 = jnp.float32
BF16 = jnp.bfloat16

LAYOUTS = (
    ((1, 1), (1, 1), (1, 0), (1, 0), (0, 1), (0, 0)),
    ((1, 1), (1, 1), (1, 0), (1, 0), (0, 1), (0, 1)),
    ((1, 1), (1, 1), (1, 1), (1, 0), (0, 1), (0, 0)),
    ((1, 1),) * 6,
)


def halves(tile):
    turned = jnp.transpose(tile)
    return jnp.concatenate([turned[:, :128], turned[:, 128:]], axis=0)


def plan_kernel(window, order, reach, choice, kinds, sizes, places):
    def measure(h, counts):
        sides = [window[h, 0, j] for j in (4, 28, 12, 20)]
        columns = window[h, 0, 17] + window[h, 0, 18] + window[h, 0, 19]
        for j, value in enumerate(sides + [columns]):
            sizes[h * 5 + j] = value
        frame = jnp.maximum(sides[0], sides[1])
        row = jnp.maximum(sides[2], sides[3])
        kind = jnp.where(frame > 0, 1 - row, 3 - row)
        kinds[h] = kind
        return tuple(whole + jnp.where(kind == k, 1, 0) for k, whole in enumerate(counts))

    many = lax.fori_loop(0, H, measure, (jnp.int32(0),) * 4, unroll=12)
    best = jnp.int32(len(LAYOUTS) - 1)
    for number in reversed(range(len(LAYOUTS) - 1)):
        layout = LAYOUTS[number]
        both = COLS * sum(f and r for f, r in layout)
        frames = COLS * sum(f for f, _ in layout)
        rows = COLS * sum(r and not f for f, r in layout)
        first_rows = many[0] + many[1] + many[2]
        fits = (many[0] <= both) & (many[0] + many[1] <= frames) & (first_rows <= frames + rows)
        fits = fits & ((many[2] == 0) | (many[0] + many[1] == frames))
        best = jnp.where(fits, number, best)
    choice[0] = best
    start = jnp.int32(0)
    for k in range(4):
        places[k] = start
        start = start + many[k]

    def deal(h, _):
        kind = kinds[h]
        place = places[kind]
        places[kind] = place + 1
        order[place] = h
        return 0

    lax.fori_loop(0, H, deal, 0, unroll=12)
    lane = lax.axis_index("head")
    for s in range(SLOTS):
        head = order[s * COLS + lane]
        for j in range(5):
            reach[s * 5 + j] = sizes[head * 5 + j]
    for j in range(5):
        reach[SLOTS * 5 + j] = 0


def make_plan(window_mask):
    smem = pl.BlockSpec(memory_space=pltpu.SMEM)
    return pl.pallas_call(
        plan_kernel,
        out_shape=(
            jax.ShapeDtypeStruct((H,), jnp.int32),
            jax.ShapeDtypeStruct((SLOTS * 5 + 5,), jnp.int32),
            jax.ShapeDtypeStruct((1,), jnp.int32),
        ),
        in_specs=[smem],
        out_specs=(smem, smem, smem),
        scratch_shapes=[
            pltpu.SMEM((H,), jnp.int32),
            pltpu.SMEM((H * 5,), jnp.int32),
            pltpu.SMEM((4,), jnp.int32),
        ],
        name="plan",
    )(window_mask)


def timetable(layout):
    wide_rows = sum(frame and row for frame, row in layout) == 3
    y_time, z_time, x_time = (9.5, 12.0, 6.5) if wide_rows else (9.0, 13.0, 7.0)
    block_time, end_time = 1.3, 0.8
    events, z_free, x_ready = [], 0.0, []
    for s, (has_frame, has_row) in enumerate(layout):
        y_done = y_time * (s + 1) + 1
        events.append((y_done, ("y", s), ((s, 4),)))
        if has_frame:
            z_free = max(z_free, y_done) + z_time
            events.append((z_free, ("z", s), ((s, 1), (s, 7))))
        if has_row:
            x_ready.append((y_done, ("xc", s), ((s, 3), (s, 5)), x_time))
            if has_frame:
                x_ready.append((z_free, ("xk", s), ((s, 0), (s, 2), (s, 6), (s, 8)), 2 * x_time))
    x_free = 0.0
    for ready, name, jobs, length in sorted(x_ready):
        x_free = max(x_free, ready) + length
        events.append((x_free, name, jobs))
    events.sort()
    steps, waits, open_jobs, now = [], [], [], 0.0
    while events or open_jobs:
        while events and (events[0][0] <= now or not open_jobs):
            at, name, jobs = events.pop(0)
            now = max(now, at)
            waits.append(name)
            open_jobs.extend(jobs)
        open_jobs.sort(key=lambda job: (-job[0] if wide_rows else job[0], job[1] != 4))
        job = open_jobs.pop(0)
        steps.append((tuple(waits), job))
        waits = []
        now += block_time
        if not any(later[0] == job[0] for _, _, jobs in events for later in jobs) and not any(
                later[0] == job[0] for later in open_jobs):
            now += end_time
    return steps


def fused_kernel(
    layout, order, reach, q_in, k_in, v_in, back, raw, pack, q_held, kv_held, held, total, top, waiting, result,
    raw_sem, own_sem, y_send, y_recv, z_send, z_recv, x_send, x_recv, o_own, o_send, o_recv,
):
    frame = lax.axis_index("frame")
    lane = lax.axis_index("head")
    ftile, row = frame // ROWS, lax.rem(frame, ROWS)
    has = {
        ("z", 1): ftile < FTILES - 1,
        ("z", -1): ftile > 0,
        ("x", 1): row < ROWS - 1,
        ("x", -1): row > 0,
    }
    hop = {"z": ROWS, "x": 1}
    mesh_ids = pl.DeviceIdType.MESH
    lanes = (1, 3, 2)

    def at(axis, way):
        return {"frame": frame + way * hop[axis], "head": lane}

    def across(step):
        return {"frame": frame, "head": lax.rem(lane + step, COLS)}

    barrier = pltpu.get_barrier_semaphore()
    for step in lanes:
        pl.semaphore_signal(barrier, inc=1, device_id=across(step), device_id_type=mesh_ids)
    peers = jnp.int32(3)
    for (axis, way), there in has.items():
        peers = peers + jnp.where(there, 1, 0)

        @pl.when(there)
        def _(axis=axis, way=way):
            pl.semaphore_signal(barrier, inc=1, device_id=at(axis, way), device_id_type=mesh_ids)

    def raw_copies(h):
        column = pl.ds(pl.multiple_of(h * HEAD_DIM, HEAD_DIM), HEAD_DIM)
        return [
            pltpu.make_async_copy(source.at[:, column], raw.at[i, h], raw_sem.at[i, h])
            for i, source in enumerate((q_in, k_in, v_in))
        ]

    def load_raw(h, _):
        for copy in raw_copies(h):
            copy.start()
        return 0

    def wait_raw(h, _):
        for copy in raw_copies(h):
            copy.wait()
        return 0

    def pack_slot(s):
        def one(y, _):
            head = order[s * COLS + y]
            pack[s, y, 0] = halves(raw[0, head])
            pack[s, y, 1] = raw[1, head]
            pack[s, y, 2] = halves(raw[2, head])
            return 0

        lax.fori_loop(0, COLS, one, 0)

    def own_copies(s):
        return (
            pltpu.make_async_copy(pack.at[s, lane, 0], q_held.at[s * COLS + lane], own_sem.at[s, 0]),
            pltpu.make_async_copy(pack.at[s, lane, pl.ds(1, 2)], kv_held.at[s * 9 + 4, :, lane], own_sem.at[s, 1]),
        )

    def y_copies(s, step):
        peer = lax.rem(lane + step, COLS)
        return (
            pltpu.make_async_remote_copy(
                src_ref=pack.at[s, peer, pl.ds(1, 2)], dst_ref=kv_held.at[s * 9 + 4, :, lane],
                send_sem=y_send.at[s, step - 1, 1], recv_sem=y_recv.at[s, step - 1, 1],
                device_id=across(step), device_id_type=mesh_ids),
            pltpu.make_async_remote_copy(
                src_ref=pack.at[s, peer, 0], dst_ref=q_held.at[s * COLS + lane],
                send_sem=y_send.at[s, step - 1, 0], recv_sem=y_recv.at[s, step - 1, 0],
                device_id=across(step), device_id_type=mesh_ids),
        )

    def z_copy(s, way):
        side = 0 if way == 1 else 1
        return pltpu.make_async_remote_copy(
            src_ref=kv_held.at[s * 9 + 4], dst_ref=kv_held.at[s * 9 + (1 - way) * 3 + 1],
            send_sem=z_send.at[s, side], recv_sem=z_recv.at[s, side],
            device_id=at("z", way), device_id_type=mesh_ids)

    def x_copy(s, f, way):
        side = 0 if way == 1 else 1
        return pltpu.make_async_remote_copy(
            src_ref=kv_held.at[s * 9 + f * 3 + 1], dst_ref=kv_held.at[s * 9 + f * 3 + 1 - way],
            send_sem=x_send.at[s, f, side], recv_sem=x_recv.at[s, f, side],
            device_id=at("x", way), device_id_type=mesh_ids)

    def o_copy(s, step):
        peer = lax.rem(lane + step, COLS)
        return pltpu.make_async_remote_copy(
            src_ref=result.at[s * COLS + peer], dst_ref=back.at[s * COLS + lane],
            send_sem=o_send.at[s, step - 1], recv_sem=o_recv.at[s, step - 1],
            device_id=across(step), device_id_type=mesh_ids)

    def o_keep(s):
        return pltpu.make_async_copy(result.at[s * COLS + lane], back.at[s * COLS + lane], o_own.at[s])

    def present(f):
        return True if f == 1 else has[("z", -1 if f == 0 else 1)]

    def when_row(f, way, act):
        @pl.when(jnp.logical_and(has[("x", way)], present(f)))
        def _():
            act()

    def start_y(s):
        for copy in own_copies(s):
            copy.start()
        for step in lanes:
            for copy in y_copies(s, step):
                copy.start()

    def wait(kind, s):
        has_frame, has_row = layout[s]
        if kind == "y":
            for copy in own_copies(s):
                copy.wait()
            for step in lanes:
                for copy in y_copies(s, step):
                    copy.wait_recv()
            if s + 2 < SLOTS:
                start_y(s + 2)
            for way in (1, -1):
                if has_frame:
                    @pl.when(has[("z", way)])
                    def _(way=way):
                        z_copy(s, way).start()
                if has_row:
                    when_row(1, way, lambda way=way: x_copy(s, 1, way).start())
        elif kind == "z":
            for way in (1, -1):
                @pl.when(has[("z", -way)])
                def _(way=way):
                    z_copy(s, way).wait_recv()
            if has_row:
                for f in (0, 2):
                    for way in (1, -1):
                        when_row(f, way, lambda f=f, way=way: x_copy(s, f, way).start())
        else:
            for f in (1,) if kind == "xc" else (0, 2):
                for way in (1, -1):
                    when_row(f, -way, lambda f=f, way=way: x_copy(s, f, way).wait_recv())

    def wide(tile):
        return jnp.concatenate([tile[:128], tile[128:]], axis=1)

    def first(s, c, block, allowed):
        q_turned = wide(q_held[s * COLS + c])
        largest = None
        for t in range(COLS):
            part = jnp.dot(kv_held[block, 0, t], q_turned, preferred_element_type=F32)
            held[c, t * TILE:(t + 1) * TILE, :] = part
            part = jnp.max(part.reshape(TILE // 8, 8, TILE), axis=0)
            part = jnp.where(allowed[abs(t - c)], part, -jnp.inf)
            largest = part if largest is None else jnp.maximum(largest, part)
        return jnp.max(largest, axis=0, keepdims=True)

    def second(s, c, block, allowed, largest, fresh):
        item = s * COLS + c
        before = jnp.where(fresh, -1e30, top[item, 0:1, :])
        row_top = jnp.maximum(before, largest)
        shift = row_top * SCALE2
        summed = jnp.where(fresh, 0.0, total[item]) * jnp.exp2((before - row_top) * SCALE2)
        for t in range(COLS):
            shift_here = jnp.where(allowed[abs(t - c)], shift, jnp.inf)
            weights = jnp.exp2(held[c, t * TILE:(t + 1) * TILE, :] * SCALE2 - shift_here).astype(BF16)
            values = jnp.concatenate([wide(kv_held[block, 1, t]), jnp.ones((16, TILE), BF16)], axis=0)
            summed = summed + jnp.dot(values, weights, preferred_element_type=F32)
        total[item] = summed
        top[item, 0:1, :] = row_top

    def gates(s, b):
        f, r = b // 3, lax.rem(b, 3)
        base = s * 5
        flag = jnp.where(f == 1, 1, jnp.where(f == 0, reach[base], reach[base + 1]))
        flag = flag * jnp.where(r == 1, 1, jnp.where(r == 0, reach[base + 2], reach[base + 3]))
        columns = jnp.where(flag > 0, reach[base + 4], -1)
        return [columns >= gap for gap in range(COLS)]

    def finish_last_column(s, b):
        second(s, COLS - 1, jnp.where(s == SLOTS, 4, s * 9 + b), gates(s, b), waiting[0:1, :], b == 4)

    def attend_block(s, b, s_before, b_before):
        allowed = gates(s, b)
        block = s * 9 + b
        largest = first(s, 0, block, allowed)
        finish_last_column(s_before, b_before)
        for c in range(COLS - 1):
            following = first(s, c + 1, block, allowed)
            second(s, c, block, allowed, largest, b == 4)
            largest = following
        waiting[0:1, :] = largest

    steps = timetable(layout)
    last_of = {s: i for i, (_, (s, _)) in enumerate(steps)}

    def pick(i, values):
        chosen = jnp.int32(values[0])
        for number, value in enumerate(values):
            if number and value != values[0]:
                chosen = jnp.where(i == number, value, chosen)
        return chosen

    def run_step(i, pending):
        for number, (waits, _) in enumerate(steps):
            if waits:
                @pl.when(i == number)
                def _(waits=waits):
                    for kind, s in waits:
                        wait(kind, s)
        s = pick(i, [job[0] for _, job in steps])
        b = pick(i, [job[1] for _, job in steps])
        f, r = b // 3, lax.rem(b, 3)
        inside = jnp.logical_and(
            jnp.logical_and(ftile + f >= 1, ftile + f <= FTILES), jnp.logical_and(row + r >= 1, row + r <= ROWS))

        @pl.when(inside)
        def _():
            attend_block(s, b, *pending)

        pending = tuple(jnp.where(inside, new, old) for new, old in zip((s, b), pending))
        done = pick(i, [int(last_of[job[0]] == number) for number, (_, job) in enumerate(steps)]) == 1

        @pl.when(done)
        def _():
            finish_last_column(*pending)
            for c in range(COLS):
                summed = total[s * COLS + c]
                blended = summed[:HEAD_DIM] / summed[HEAD_DIM:HEAD_DIM + 1]
                result[s * COLS + c] = jnp.transpose(blended).astype(BF16)
            o_keep(s).start()
            for step in lanes:
                o_copy(s, step).start()

        return jnp.where(done, SLOTS, pending[0]), jnp.where(done, 4, pending[1])

    lax.fori_loop(0, H, load_raw, 0)
    waiting[...] = jnp.zeros_like(waiting)
    held[COLS - 1] = jnp.zeros((COLS * TILE, TILE), F32)
    lax.fori_loop(0, H, wait_raw, 0)
    pack_slot(0)
    pl.semaphore_wait(barrier, peers)
    start_y(0)
    pack_slot(1)
    start_y(1)
    for s in range(2, SLOTS):
        pack_slot(s)
    lax.fori_loop(0, len(steps), run_step, (jnp.int32(SLOTS), jnp.int32(4)))

    for s, (has_frame, has_row) in enumerate(layout):
        o_keep(s).wait()
        for step in lanes:
            o_copy(s, step).wait()
            for copy in y_copies(s, step):
                copy.wait_send()
        for way in (1, -1):
            if has_frame:
                @pl.when(has[("z", way)])
                def _(s=s, way=way):
                    z_copy(s, way).wait_send()
            if has_row:
                for f in (0, 1, 2) if has_frame else (1,):
                    when_row(f, way, lambda s=s, f=f, way=way: x_copy(s, f, way).wait_send())


def fused(number, order, reach, queries, key_rows, value_rows):
    dma = pltpu.SemaphoreType.DMA
    smem = pl.BlockSpec(memory_space=pltpu.SMEM)
    any_space = pl.BlockSpec(memory_space=pl.ANY)
    items = SLOTS * COLS
    return pl.pallas_call(
        functools.partial(fused_kernel, LAYOUTS[number]),
        out_shape=jax.ShapeDtypeStruct((items, TILE, HEAD_DIM), BF16),
        in_specs=[smem, smem, any_space, any_space, any_space],
        out_specs=any_space,
        scratch_shapes=[
            pltpu.VMEM((3, H, TILE, HEAD_DIM), BF16),
            pltpu.VMEM((SLOTS, COLS, 3, TILE, HEAD_DIM), BF16),
            pltpu.VMEM((items, TILE, HEAD_DIM), BF16),
            pltpu.VMEM((SLOTS * 9, 2, COLS, TILE, HEAD_DIM), BF16),
            pltpu.VMEM((COLS, COLS * TILE, TILE), F32),
            pltpu.VMEM((items + COLS, HEAD_DIM + 16, TILE), F32),
            pltpu.VMEM((items + COLS, 8, TILE), F32),
            pltpu.VMEM((8, TILE), F32),
            pltpu.VMEM((items, TILE, HEAD_DIM), BF16),
            dma((3, H)),
            dma((SLOTS, 2)),
            dma((SLOTS, 3, 2)),
            dma((SLOTS, 3, 2)),
            dma((SLOTS, 2)),
            dma((SLOTS, 2)),
            dma((SLOTS, 3, 2)),
            dma((SLOTS, 3, 2)),
            dma((SLOTS,)),
            dma((SLOTS, 3)),
            dma((SLOTS, 3)),
        ],
        compiler_params=pltpu.CompilerParams(
            collective_id=number, has_side_effects=True, vmem_limit_bytes=60 * 2**20
        ),
        name="fused",
    )(order, reach, queries, key_rows, value_rows)


def place_kernel(order, back_ref, o_ref):
    def one(i, _):
        column = pl.ds(pl.multiple_of(order[i] * HEAD_DIM, HEAD_DIM), HEAD_DIM)
        o_ref[:, column] = back_ref[i]
        return 0
    lax.fori_loop(0, H, one, 0, unroll=8)


def place(order, back):
    return pl.pallas_call(
        place_kernel,
        out_shape=jax.ShapeDtypeStruct((TILE, H * HEAD_DIM), BF16),
        in_specs=[pl.BlockSpec(memory_space=pltpu.SMEM), pl.BlockSpec(memory_space=pltpu.VMEM)],
        out_specs=pl.BlockSpec(memory_space=pltpu.VMEM),
        name="place",
    )(order, back)


def per_device(queries, key_rows, value_rows, window_mask):
    order, reach, choice = make_plan(window_mask)
    back = lax.switch(
        choice[0], [functools.partial(fused, number) for number in range(len(LAYOUTS))],
        order, reach, queries, key_rows, value_rows,
    )
    return place(order, back)


def solution(mesh):
    return jax.shard_map(
        per_device,
        mesh=mesh,
        in_specs=(
            P(("frame", "head"), None),
            P(("frame", "head"), None),
            P(("frame", "head"), None),
            P(None, "frame", None),
        ),
        out_specs=P(("frame", "head"), None),
        check_vma=False,
    )
```
